32 devices in a mesh: dp: 8 (over y, x, core), tensor: 4 (over z).
Axes of the slice: x: 2, y: 2, z: 4, core: 2. Of those that a mesh axis runs over, the one named last changes fastest.
Arguments:
- tokens: bfloat16 [32, 200, 768], P(('dp', 'tensor')), may hold values from -6 to 6
- gain_first: float32 [768], replicated, may hold values from 0.25 to 1.75
- qkv_weight: bfloat16 [3, 768, 768], P(None, 'dp', 'tensor'), may hold values from -0.21875 to 0.21875
- out_weight: bfloat16 [768, 768], P('tensor', 'dp'), may hold values from -2 to 2
- gain_second: float32 [768], replicated, may hold values from 0.25 to 1.75
- router_weight: bfloat16 [768, 3], replicated, may hold values from -0.15625 to 0.15625
- expert_in: bfloat16 [3, 768, 3072], P(None, 'dp', 'tensor'), may hold values from -0.21875 to 0.21875
- expert_out: bfloat16 [3, 3072, 768], P(None, 'tensor', 'dp'), may hold values from -0.3125 to 0.3125
- routes: int32 [32, 200, 2], P('dp'), may hold values from 0 to 2, as said below
- slot_index: int32 [32, 200, 2], P('dp'), may hold values from 0 to 525, as said below
- cotangent: bfloat16 [32, 200, 768], P(('dp', 'tensor')), may hold values from -6 to 6
Outputs:
- output: bfloat16 [32, 200, 768], P(('dp', 'tensor'))
- grad_tokens: float32 [32, 200, 768], P(('dp', 'tensor'))
- grad_gain_first: float32 [768], replicated
- grad_qkv_weight: float32 [3, 768, 768], P(None, 'dp', 'tensor')
- grad_out_weight: float32 [768, 768], P('tensor', 'dp')
- grad_gain_second: float32 [768], replicated
- grad_router_weight: float32 [768, 3], replicated
- grad_expert_in: float32 [3, 768, 3072], P(None, 'dp', 'tensor')
- grad_expert_out: float32 [3, 3072, 768], P(None, 'tensor', 'dp')
The draws below stay inside these ranges and needn't reach their ends.
Inputs may be any that keep to these rules, and one draw needn't show every extreme that they name: `routes`: the 2 entries of a token are different experts. `slot_index`: within the 4 images of one index of dp, slots follow the order of arrival: all first routes in token order, then all second routes; a route at a position below 197 gets the number of earlier such routes to its expert, or 525 when that number is 525 or more (a dropped route); positions 197 and beyond always carry 525. So no two kept routes of one group share an expert and a slot.
All inputs are finite; a program needn't handle non-finite values.
Results may differ from the reference program's by a relative error of at most 0.017.
Values may be sent and summed in bfloat16 or wider, within the bound.
No kernel may reach another device: no remote copies, remote signals or barrier semaphores. Data moves between devices by JAX's collectives and lax.ppermute only.
A program may use at most 128 MiB of HBM per device.

```python
import math
import jax
import jax.numpy as jnp
from jax import lax

D = 768
HEADS = 12
HD = 64
FF = 3072
EXPERTS = 3
TOPK = 2
SEQ = 200
IMG_DEV = 4
VALID = 197
IMAGES = 32
CAP = 525


def route_table(key):
    group_count = IMAGES // IMG_DEV
    row_count = IMG_DEV * SEQ
    first_pick = jax.random.randint(jax.random.fold_in(key, 11), (group_count, row_count), 0, EXPERTS)
    step_pick = jax.random.randint(jax.random.fold_in(key, 12), (group_count, row_count), 1, EXPERTS)
    second_pick = (first_pick + step_pick) % EXPERTS
    route_rows = jnp.stack([first_pick, second_pick], axis=-1)
    position = jnp.arange(row_count, dtype=jnp.int32) % SEQ
    valid_rows = position < VALID
    arrival = jnp.concatenate([first_pick, second_pick], axis=1)
    live_rows = jnp.concatenate([valid_rows, valid_rows])[None, :]
    hits = (arrival[:, :, None] == jnp.arange(EXPERTS, dtype=jnp.int32)[None, None, :]) & live_rows[:, :, None]
    ranks = jnp.cumsum(hits.astype(jnp.int32), axis=1) - 1
    slot_rows = jnp.sum(jnp.where(hits, ranks, 0), axis=-1)
    slot_rows = jnp.where(live_rows & (slot_rows < CAP), slot_rows, CAP)
    slot_pairs = jnp.stack([slot_rows[:, :row_count], slot_rows[:, row_count:]], axis=-1)
    return (route_rows.reshape(IMAGES, SEQ, TOPK).astype(jnp.int32), slot_pairs.reshape(IMAGES, SEQ, TOPK).astype(jnp.int32))


def draw_routes(key, part):
    shared = route_table(key)
    return shared[0]


def draw_slot_index(key, part):
    shared = route_table(key)
    return shared[1]


def shard_levels(stream_key, shape, cuts, smallest, largest):
    factor_of, own = 1.0, jax.random.fold_in(stream_key, 6)
    for axis_at, blocks in cuts:
        steps = jnp.exp(jax.random.uniform(jax.random.fold_in(own, axis_at), (blocks,), jnp.float32, smallest / len(cuts), largest / len(cuts)))
        factor_of = factor_of * jnp.repeat(steps, shape[axis_at] // blocks).reshape([-1 if axis == axis_at else 1 for axis in range(len(shape))])
    return factor_of


def scatter_about(key, shape, deviation, reach, shards=(), held_as=jnp.bfloat16):
    loudness = shard_levels(key, shape, shards, -0.22, 0.18) if shards else 1.0
    array = jax.random.normal(key, shape, jnp.float32) * deviation * loudness
    return jnp.minimum(jnp.maximum(array, -reach), reach).astype(held_as)


def setup_inputs(seed: int = 0) -> dict:
    keys = jax.random.split(jax.random.key(seed), 12)
    tokens = scatter_about(keys[0], (IMAGES, SEQ, D), 1.0, 6.0, ((0, 32),))
    gain_first = jnp.clip(1.0 + 0.15 * jax.random.normal(keys[1], (D,), jnp.float32), 0.25, 1.75)
    qkv_weight = scatter_about(keys[2], (3, D, HEADS * HD), D ** -0.5, 0.21875, ((1, 8), (2, 4)))
    out_weight = scatter_about(keys[3], (HEADS * HD, D), (HEADS * HD * 2 // SEQ) ** -0.5, 2.0, ((0, 4), (1, 8)))
    gain_second = jnp.clip(1.0 + 0.15 * jax.random.normal(keys[4], (D,), jnp.float32), 0.25, 1.75)
    router_weight = scatter_about(keys[5], (D, EXPERTS), (2 * D) ** -0.5, 0.15625)
    expert_in = scatter_about(keys[6], (EXPERTS, D, FF), D ** -0.5, 0.21875, ((1, 8), (2, 4)))
    expert_out = scatter_about(keys[7], (EXPERTS, FF, D), (FF // 8) ** -0.5, 0.3125, ((1, 4), (2, 8)))
    routes = draw_routes(jax.random.fold_in(keys[11], 71), 0)
    slot_index = draw_slot_index(jax.random.fold_in(keys[11], 71), 0)
    cotangent = scatter_about(keys[10], (IMAGES, SEQ, D), 1.0, 6.0, ((0, 32),))
    return {"tokens": tokens, "gain_first": gain_first, "qkv_weight": qkv_weight, "out_weight": out_weight, "gain_second": gain_second, "router_weight": router_weight, "expert_in": expert_in, "expert_out": expert_out, "routes": routes, "slot_index": slot_index, "cotangent": cotangent}


@jax.custom_vjp
def low(v):
    return lax.optimization_barrier(v.astype(jnp.bfloat16)).astype(jnp.float32)

@jax.custom_vjp
def low_back(v):
    return v

def low_keep(v):
    return (low(v), None)

def low_pass(kept, grad):
    return (grad,)

def back_keep(v):
    return (v, None)

def back_low(kept, grad):
    return (low(grad),)
low.defvjp(low_keep, low_pass)
low_back.defvjp(back_keep, back_low)
EPSILON = 1e-06
NEGATIVE = -1e+30
HIGHEST = lax.Precision.HIGHEST

def layer_norm(values, gain):
    centered = values - lax.optimization_barrier(jnp.mean(values, axis=-1, keepdims=True))
    variance = lax.optimization_barrier(jnp.mean(centered * centered, axis=-1, keepdims=True))
    return centered * lax.rsqrt(variance + EPSILON) * gain

def attend_block(normed, qkv_weight, out_weight):
    image_count = normed.shape[0]
    packed = low(low_back(jnp.einsum('bsd,cdh->cbsh', normed, qkv_weight, precision=HIGHEST)))
    head_shape = (image_count, SEQ, HEADS, HD)
    query_rows = packed[0].reshape(head_shape)
    key_rows = packed[1].reshape(head_shape)
    value_rows = packed[2].reshape(head_shape)
    raw_scores = low_back(jnp.einsum('bqhd,bkhd->bhqk', query_rows, key_rows, precision=HIGHEST) * HD ** (-0.5))
    valid_keys = jnp.arange(SEQ) < VALID
    soft_low = low(jax.nn.softmax(jnp.where(valid_keys, raw_scores, NEGATIVE), axis=-1))
    mixed_rows = jnp.einsum('bhqk,bkhd->bqhd', soft_low, value_rows, precision=HIGHEST)
    mixed_rows = low(low_back(mixed_rows.reshape(image_count, SEQ, HEADS * HD)))
    return low_back(jnp.einsum('bsh,hd->bsd', mixed_rows, out_weight, precision=HIGHEST))

def expert_group(group_items, expert_in, expert_out):
    normed, route_rows, slot_rows, weight, live_mask = group_items
    row_count = normed.shape[0]
    placed = jnp.where(live_mask, route_rows * CAP + slot_rows, EXPERTS * CAP).astype(jnp.int32)
    owner_rows = jnp.broadcast_to(jnp.arange(row_count, dtype=jnp.int32)[:, None], placed.shape)
    slot_table = jnp.full((EXPERTS * CAP + 1,), row_count, jnp.int32).at[placed.reshape(-1)].set(owner_rows.reshape(-1))
    padded = jnp.concatenate([normed, jnp.zeros((1, D), normed.dtype)], axis=0)
    entering = padded[slot_table[:EXPERTS * CAP]].reshape(EXPERTS, CAP, D)
    pre_act = low_back(jnp.einsum('ecd,edf->ecf', entering, expert_in, precision=HIGHEST))
    hidden = low(jax.nn.gelu(pre_act, approximate=False))
    leaving = low_back(jnp.einsum('ecf,efd->ecd', hidden, expert_out, precision=HIGHEST))
    flat_rows = jnp.concatenate([leaving.reshape(EXPERTS * CAP, D), jnp.zeros((1, D), leaving.dtype)], axis=0)
    return lax.optimization_barrier(jnp.sum(weight[:, :, None] * flat_rows[placed], axis=1))

def forward(tokens, gain_first, qkv_weight, out_weight, gain_second, router_weight, expert_in, expert_out, routes, slot_index):
    block_size = math.gcd(IMAGES, 16)
    first_norm = low(layer_norm(tokens, gain_first))

    def attend(first_block):
        return attend_block(first_block, qkv_weight, out_weight)
    attended = lax.map(jax.checkpoint(attend), first_norm.reshape(IMAGES // block_size, block_size, SEQ, D))
    residual = tokens + attended.reshape(IMAGES, SEQ, D)
    second_norm = low(layer_norm(residual, gain_second))
    logits = low_back(jnp.einsum('isd,de->ise', second_norm, router_weight, precision=HIGHEST))
    gate_probs = jax.nn.softmax(logits, axis=-1)
    live_mask = (slot_index < CAP) & (jnp.arange(SEQ) < VALID)[None, :, None]
    weight = jnp.where(live_mask, jnp.take_along_axis(gate_probs, routes, axis=-1), 0.0)
    group_count = IMAGES // IMG_DEV
    row_count = IMG_DEV * SEQ

    def route_group(group_items):
        return expert_group(group_items, expert_in, expert_out)
    group_items = (second_norm.reshape(group_count, row_count, D), routes.reshape(group_count, row_count, TOPK), slot_index.reshape(group_count, row_count, TOPK), weight.reshape(group_count, row_count, TOPK), live_mask.reshape(group_count, row_count, TOPK))
    branch = lax.map(jax.checkpoint(route_group), group_items).reshape(IMAGES, SEQ, D)
    return residual + low_back(branch)

def reference(tokens, gain_first, qkv_weight, out_weight, gain_second, router_weight, expert_in, expert_out, routes, slot_index, cotangent):
    floats = (tokens.astype(jnp.float32), gain_first.astype(jnp.float32), qkv_weight.astype(jnp.float32), out_weight.astype(jnp.float32), gain_second.astype(jnp.float32), router_weight.astype(jnp.float32), expert_in.astype(jnp.float32), expert_out.astype(jnp.float32))

    def forward_pass(*weights):
        return forward(*weights, routes, slot_index)
    outcome, pullback = jax.vjp(forward_pass, *floats)
    gradients = pullback(cotangent.astype(jnp.float32))
    return (outcome.astype(jnp.bfloat16), gradients[0], gradients[1], gradients[2], gradients[3], gradients[4], gradients[5], gradients[6], gradients[7])
```

```python
import functools

import jax
import jax.numpy as jnp
from jax import lax
from jax.experimental import pallas as pl
from jax.experimental.pallas import tpu as pltpu
from jax.sharding import PartitionSpec as P

HD = 64
VALID = 197
CAP = 525
LANES = 128
EPSILON = 1e-06
NEGATIVE = -1e30
F32 = jnp.float32
BF16 = jnp.bfloat16
VMEM_LIMIT = 58 * 1024 * 1024

KEEP = (0, 2, 4, 6)
SEND = (1, 3, 5, 7)


def nn(a, b):
    return lax.dot_general(a, b, (((1,), (0,)), ((), ())), preferred_element_type=F32)


def nt(a, b):
    return lax.dot_general(a, b, (((1,), (1,)), ((), ())), preferred_element_type=F32)


def tn(a, b):
    return lax.dot_general(a, b, (((0,), (0,)), ((), ())), preferred_element_type=F32)


def norm_parts(values):
    centered = values - jnp.mean(values, axis=-1, keepdims=True)
    variance = jnp.mean(centered * centered, axis=-1, keepdims=True)
    inverse = lax.rsqrt(variance + EPSILON)
    return centered * inverse, inverse


def norm_backward(xhat, inverse, grad, gain):
    h = grad * gain
    mean_h = jnp.mean(h, axis=-1, keepdims=True)
    mean_hx = jnp.mean(h * xhat, axis=-1, keepdims=True)
    return inverse * (h - mean_h - xhat * mean_hx)


def shift(x, axis, size, distance):
    return lax.ppermute(x, axis, [(i, i ^ distance) for i in range(size)])


def after(x, *others):
    return lax.optimization_barrier((x,) + others)[0]


def gather_dp(x, size):
    n = x.shape[0]
    if size != 8:
        full = lax.all_gather(x, "dp", axis=1, tiled=True)
        return [(full, 0, 0)]
    half = n // 2
    from_x = shift(x, "dp", size, 2)
    from_y = shift(x, "dp", size, 4)
    low = shift(from_x[:half], "dp", size, 4)
    high = shift(from_y[half:], "dp", size, 2)
    mine = [(x, 0, 0), (from_x, 0, 2), (from_y, 0, 4), (low, 0, 6), (high, half, 6)]
    return mine + [(shift(a, "dp", size, 1), lo, rel ^ 1) for a, lo, rel in mine]


def reduce_dp(keep, send, size):
    if size != 8:
        return lax.psum_scatter(keep[0], "dp", scatter_dimension=1, tiled=True).astype(F32)
    n = keep.shape[1]
    half = n // 2
    arrived = shift(send, "dp", size, 1)
    total = [keep[j].astype(F32) + arrived[j].astype(F32) for j in range(4)]
    far = total[3].astype(BF16)
    low = shift(far[:half], "dp", size, 2).astype(F32)
    high = shift(far[half:], "dp", size, 4).astype(F32)
    to_x = jnp.concatenate([total[1][:half], total[1][half:] + high]).astype(BF16)
    to_y = jnp.concatenate([total[2][:half] + low, total[2][half:]]).astype(BF16)
    from_x = shift(to_x, "dp", size, 2).astype(F32)
    from_y = shift(to_y, "dp", size, 4).astype(F32)
    return total[0] + from_x + from_y


def start_pieces(layout, refs, where, offs, rows, sems, base=0):
    copies = []
    for ref, (lo, count, rel) in zip(refs, layout):
        spot = pl.multiple_of(offs[rel], 16)
        copy = pltpu.make_async_copy(
            ref, where.at[pl.ds(lo, count), pl.ds(spot, rows), :], sems.at[base + len(copies)]
        )
        copy.start()
        copies.append(copy)
    return copies


def attention_forward(layout, rows, count, offs, tokens, gain1, gain2, *rest):
    pieces = rest[:count]
    resid, second, first, qk_out, v_out, mixed_out, weights, sems = rest[count:]
    copies = start_pieces(layout, pieces, weights, offs, rows, sems)
    wide = tokens[...].astype(F32)
    xhat, _ = norm_parts(wide)
    fn = (xhat * gain1[...]).astype(BF16)
    first[...] = fn
    seq = fn.shape[0]
    for copy in copies:
        copy.wait()
    keys = lax.broadcasted_iota(jnp.int32, (seq, seq), 1) < VALID
    groups = weights.shape[0] // 2
    cols = weights.shape[2] // 2
    total = wide
    for g in range(groups):
        qk = nn(fn, weights[2 * g]).astype(BF16)
        v = nn(fn, weights[2 * g + 1])[:, :cols].astype(BF16)
        qk_out[g] = qk
        v_out[g] = v
        mixed = [jnp.zeros((seq, cols), BF16)]
        for h in range(cols // HD):
            q = qk[:, h * HD : (h + 1) * HD]
            k = qk[:, cols + h * HD : cols + (h + 1) * HD]
            s = jnp.where(keys, nt(q, k) * (HD**-0.5), NEGATIVE)
            e = jnp.exp(s - jnp.max(s, axis=-1, keepdims=True))
            p = e / jnp.sum(e, axis=-1, keepdims=True)
            mixed.append(nn(p.astype(BF16), v[:, h * HD : (h + 1) * HD]).astype(BF16))
        mixed = jnp.concatenate(mixed, axis=1)
        mixed_out[g] = mixed
        total = total + nt(mixed, weights[2 * g + 1])
    resid[...] = total
    xhat, _ = norm_parts(total)
    second[...] = (xhat * gain2[...]).astype(BF16)


def gate_softmax(second, router, experts):
    logits = nn(second, router)
    lane = lax.broadcasted_iota(jnp.int32, logits.shape, 1)
    logits = jnp.where(lane < experts, logits, NEGATIVE)
    e = jnp.exp(logits - jnp.max(logits, axis=-1, keepdims=True))
    return e / jnp.sum(e, axis=-1, keepdims=True)


def normal_cdf_pdf(x):
    z = jnp.abs(x) * 0.7071067811865476
    t = 1.0 / (1.0 + 0.3275911 * z)
    poly = t * (
        0.127414796
        + t * (-0.142248368 + t * (0.7107068705 + t * (-0.7265760135 + t * 0.5307027145)))
    )
    bell = jnp.exp(-0.5 * x * x)
    tail = poly * bell
    return jnp.where(x >= 0, 1.0 - tail, tail), bell * 0.3989422804014327


def expert_dgrad(layout, rows, counts, images, offs, router, *rest):
    experts = len(counts)
    sn = rest[:images]
    cot = rest[images : 2 * images]
    live = rest[2 * images]
    at = 2 * images + 1
    pieces = []
    for c in counts:
        pieces.append(rest[at : at + c])
        at += c
    gs_out = rest[at : at + images]
    br_out = rest[at + images : at + 2 * images]
    dpre_out, hw_out = rest[at + 2 * images : at + 2 * images + 2]
    weights, x_all, c_all, gs_acc, br_acc, w_acc, g_acc, sems = rest[at + 2 * images + 2 :]
    copies = []
    base = 0
    for e in range(experts):
        copies.append(start_pieces(layout, pieces[e], weights.at[e], offs, rows, sems, base))
        base += counts[e]
    seq = sn[0].shape[0]
    width = sn[0].shape[1]
    for j in range(images):
        x_all[pl.ds(j * seq, seq), :] = sn[j][...]
        c_all[pl.ds(j * seq, seq), :] = cot[j][...]
    for e in range(experts):
        for copy in copies[e]:
            copy.wait()

        def tile(j, carry):
            here = pl.ds(pl.multiple_of(j * seq, 16), seq)
            x = x_all[here, :]
            lane = lax.broadcasted_iota(jnp.int32, (seq, LANES), 1)
            if e == 0:
                w = gate_softmax(x, router[...], experts) * live[here, :].astype(F32)
                w_acc[here, :] = w
                g_prev = jnp.zeros((seq, LANES), F32)
            else:
                w = w_acc[here, :]
                g_prev = g_acc[here, :]
            we = w[:, e : e + 1]
            pre = nn(x, weights[e, 0])
            gh = nn(c_all[here, :], weights[e, 1])
            cdf, pdf = normal_cdf_pdf(pre)
            hidden = (pre * cdf).astype(BF16).astype(F32)
            g = jnp.sum(hidden * gh, axis=-1, keepdims=True)
            hw = (hidden * we).astype(BF16)
            dpre = (gh * we * (cdf + pre * pdf)).astype(BF16)
            hw_out[e, here, :] = hw
            dpre_out[e, here, :] = dpre
            g_acc[here, :] = jnp.where((lane == e) | (lane == e + 8), g, g_prev)
            branch = nt(hw, weights[e, 1])
            gs = nt(dpre, weights[e, 0])
            if e == 0:
                br_acc[here, :] = branch
                gs_acc[here, :] = gs
            else:
                br_acc[here, :] += branch
                gs_acc[here, :] += gs
            return carry

        lax.fori_loop(0, images, tile, 0)
    for j in range(images):
        here = pl.ds(j * seq, seq)
        gs_out[j][:, :width] = gs_acc[here, :].astype(BF16)
        g = g_acc[here, :]
        lane = lax.broadcasted_iota(jnp.int32, g.shape, 1)
        coarse = g.astype(BF16)
        gs_out[j][:, width:] = jnp.where(lane < 8, coarse.astype(F32), g - coarse.astype(F32)).astype(BF16)
        br_out[j][...] = br_acc[here, :].astype(BF16)


def put_blocks(acc, outs, blocks, index, offs, rows):
    for which, j, rel in blocks:
        spot = pl.multiple_of(offs[rel], 8)
        outs[which][(j,) + index] = acc[pl.ds(spot, rows), :].astype(BF16)


def expert_wgrad(blocks, n_out, rows, images, offs, *rest):
    sn = rest[:images]
    cot = rest[images : 2 * images]
    dpre, hw = rest[2 * images : 2 * images + 2]
    outs = rest[2 * images + 2 : 2 * images + 2 + n_out]
    acc = rest[-1]
    seq = sn[0].shape[0]
    for m, (left, right) in enumerate(((sn, dpre), (cot, hw))):
        total = None
        for j in range(images):
            part = tn(left[j][...], right[0, pl.ds(j * seq, seq), :])
            total = part if total is None else total + part
        acc[...] = total
        put_blocks(acc, outs, blocks, (m,), offs, rows)


def attention_backward(
    layout, rows, count, blocks, n_out, images, experts, out_rows,
    offs, tokens, gain1, gain2, resid, second, first, qk_in, v_in, mixed_in, live, router, cot, *rest,
):
    gs_in = rest[:images]
    pieces = rest[images : images + count]
    at = images + count
    outs = rest[at : at + n_out]
    grad_tokens, small = rest[at + n_out : at + n_out + 2]
    weights, acc, sems = rest[at + n_out + 2 :]
    copies = start_pieces(layout, pieces, weights, offs, rows, sems)
    width = second.shape[1]
    seq = second.shape[0]
    gs = gs_in[0][...].astype(F32)
    for j in range(1, images):
        gs = gs + gs_in[j][...].astype(F32)
    shares = gs[:, width:]
    gs = gs[:, :width]
    fold = (
        lax.broadcasted_iota(jnp.int32, (LANES, LANES), 0) % 8
        == lax.broadcasted_iota(jnp.int32, (LANES, LANES), 1)
    )
    lane = lax.broadcasted_iota(jnp.int32, shares.shape, 1)
    low_part = jnp.concatenate([shares[:, 8:16], jnp.zeros((seq, LANES - 8), F32)], axis=1)
    shares = jnp.where(lane < experts, shares + low_part, 0.0) * live[...].astype(F32)
    sn = second[...]
    probs = gate_softmax(sn, router[...], experts)
    inner = jnp.sum(probs * shares, axis=-1, keepdims=True)
    grad_logits = (probs * (shares - inner)).astype(BF16)
    grad_router = tn(grad_logits, sn)[:8, :]
    gs = gs + nt(grad_logits, router[...])
    xhat, inverse = norm_parts(resid[...])
    gain2_row = jnp.sum(gs * xhat, axis=0, keepdims=True)
    grad_resid = cot[...].astype(F32) + norm_backward(xhat, inverse, gs, gain2[...])
    ga = grad_resid.astype(BF16)
    fn = first[...]
    keys = lax.broadcasted_iota(jnp.int32, (seq, seq), 1) < VALID
    scale = HD**-0.5
    groups = weights.shape[0] // 2
    cols = weights.shape[2] // 2
    for copy in copies:
        copy.wait()
    grad_first = None
    for g in range(groups):
        gm = nn(ga, weights[2 * g + 1])[:, cols:].astype(BF16)
        qk = qk_in[g]
        v = v_in[g]
        grads_q, grads_k, grads_v = [], [], []
        for h in range(cols // HD):
            q = qk[:, h * HD : (h + 1) * HD]
            k = qk[:, cols + h * HD : cols + (h + 1) * HD]
            gh = gm[:, h * HD : (h + 1) * HD]
            s = jnp.where(keys, nt(q, k) * scale, NEGATIVE)
            e = jnp.exp(s - jnp.max(s, axis=-1, keepdims=True))
            p = e / jnp.sum(e, axis=-1, keepdims=True)
            grads_v.append(tn(p.astype(BF16), gh).astype(BF16))
            gp = nt(gh, v[:, h * HD : (h + 1) * HD])
            ds = (p * (gp - jnp.sum(p * gp, axis=-1, keepdims=True))).astype(BF16)
            grads_q.append((nn(ds, k) * scale).astype(BF16))
            grads_k.append((tn(ds, q) * scale).astype(BF16))
        gqk = jnp.concatenate(grads_q + grads_k, axis=1)
        gv = jnp.concatenate(grads_v + [jnp.zeros((seq, cols), BF16)], axis=1)
        acc[...] = tn(fn, gqk)
        put_blocks(acc, outs, blocks, (2 * g,), offs, rows)
        acc[...] = tn(fn, gv) + tn(ga, mixed_in[g])
        put_blocks(acc, outs, blocks, (2 * g + 1,), offs, rows)
        part = nt(gqk, weights[2 * g]) + nt(gv, weights[2 * g + 1])
        grad_first = part if grad_first is None else grad_first + part
    xhat, inverse = norm_parts(tokens[...].astype(F32))
    gain1_row = jnp.sum(grad_first * xhat, axis=0, keepdims=True)
    result = grad_resid + norm_backward(xhat, inverse, grad_first, gain1[...])
    grad_tokens[...] = result[:out_rows]
    row = lax.broadcasted_iota(jnp.int32, (8, width), 0)
    small[...] = jnp.where(row < experts, grad_router, jnp.where(row == 6, gain1_row, jnp.where(row == 7, gain2_row, 0.0)))


def call(kernel, out_shape, scratch, flops, n_bytes, name, operands, n_any, specs=None):
    total = len(operands)
    in_specs = [pl.BlockSpec(memory_space=pltpu.SMEM)]
    in_specs += [pl.BlockSpec(memory_space=pltpu.VMEM)] * (total - 1 - n_any)
    in_specs += [pl.BlockSpec(memory_space=pl.ANY)] * n_any
    if specs:
        for at, spec in specs.items():
            in_specs[at] = spec
    return pl.pallas_call(
        kernel,
        out_shape=out_shape,
        in_specs=in_specs,
        out_specs=jax.tree.map(lambda _: pl.BlockSpec(memory_space=pltpu.VMEM), out_shape),
        scratch_shapes=scratch,
        compiler_params=pltpu.CompilerParams(vmem_limit_bytes=VMEM_LIMIT),
        cost_estimate=pl.CostEstimate(flops=flops, bytes_accessed=n_bytes, transcendentals=0),
        name=name,
    )(*operands)


def on_device(
    tokens, gain_first, qkv_weight, out_weight, gain_second, router_weight,
    expert_in, expert_out, routes, slot_index, cotangent, *, dp, tensor,
):
    me = lax.axis_index("dp")
    z = lax.axis_index("tensor")
    _, seq_len, width = tokens.shape
    experts, own_rows, ff = expert_in.shape
    cols = qkv_weight.shape[2]
    seq = (seq_len + 15) // 16 * 16
    images = tensor
    split = dp == 8
    rel_count = 8 if split else 1
    rows = width // rel_count
    offs = ((me ^ jnp.arange(8, dtype=jnp.int32)) * rows) if split else jnp.zeros((8,), jnp.int32)
    offs = offs.astype(jnp.int32)
    blocks = (
        [(0, j, r) for j, r in enumerate(KEEP)] + [(1, j, r) for j, r in enumerate(SEND)]
        if split
        else [(0, 0, 0)]
    )
    n_out = 2 if split else 1
    out_lead = 4 if split else 1

    def pad_rows(x):
        return jnp.pad(x, ((0, seq - seq_len), (0, 0)))

    tok = pad_rows(tokens[0])
    cot = pad_rows(cotangent[0])
    g1 = gain_first.reshape(1, width)
    g2 = gain_second.reshape(1, width)
    router = jnp.pad(router_weight, ((0, 0), (0, LANES - experts)))

    own = jnp.stack(
        [
            jnp.concatenate([qkv_weight[0], qkv_weight[1]], axis=1),
            jnp.concatenate([qkv_weight[2], out_weight.T], axis=1),
        ]
    )
    z_pieces = [own] + [shift(own, "tensor", tensor, j) for j in range(1, tensor)]
    z_buffer = jnp.concatenate(z_pieces, axis=0)
    attn_pieces = gather_dp(z_buffer, dp)
    attn_layout = [(lo, a.shape[0], rel) for a, lo, rel in attn_pieces]
    attn_arrays = [a for a, _, _ in attn_pieces]

    cot_go = after(cot, z_buffer)
    cots = [cot] + [shift(cot_go, "tensor", tensor, j) for j in range(1, tensor)]

    token = attn_pieces[4 if split else 0][0]
    expert_arrays = []
    for e in range(experts):
        mine = after(jnp.stack([expert_in[e], expert_out[e].T]), token)
        got = gather_dp(mine, dp)
        expert_layout = [(lo, a.shape[0], rel) for a, lo, rel in got]
        expert_arrays.append([a for a, _, _ in got])
        token = got[4 if split else 0][0]

    groups = tensor
    resid, second, first, qk, v, mixed = call(
        functools.partial(attention_forward, attn_layout, rows, len(attn_arrays)),
        [
            jax.ShapeDtypeStruct((seq, width), F32),
            jax.ShapeDtypeStruct((seq, width), BF16),
            jax.ShapeDtypeStruct((seq, width), BF16),
            jax.ShapeDtypeStruct((groups, seq, 2 * cols), BF16),
            jax.ShapeDtypeStruct((groups, seq, cols), BF16),
            jax.ShapeDtypeStruct((groups, seq, 2 * cols), BF16),
        ],
        [
            pltpu.VMEM((2 * groups, width, 2 * cols), BF16),
            pltpu.SemaphoreType.DMA((len(attn_arrays),)),
        ],
        8_000_000_000, 10_000_000, "attention_forward",
        [offs, tok, g1, g2] + attn_arrays, len(attn_arrays),
    )

    seconds = [second] + [shift(second, "tensor", tensor, j) for j in range(1, tensor)]
    live = (slot_index < CAP) & (jnp.arange(seq_len) < VALID)[None, :, None]
    expert_lane = jnp.arange(LANES)
    live = jnp.any((routes[..., None] == expert_lane) & live[..., None], axis=2).astype(BF16)
    live = jnp.pad(live, ((0, 0), (0, seq - seq_len), (0, 0)))
    live = jnp.concatenate([lax.dynamic_slice_in_dim(live, z ^ j, 1, 0)[0] for j in range(images)], axis=0)

    all_rows = images * seq
    counts = [len(a) for a in expert_arrays]
    flat_experts = [a for group in expert_arrays for a in group]
    outs = call(
        functools.partial(expert_dgrad, expert_layout, rows, counts, images),
        [jax.ShapeDtypeStruct((seq, width + LANES), BF16)] * images
        + [jax.ShapeDtypeStruct((seq, width), BF16)] * images
        + [jax.ShapeDtypeStruct((experts, all_rows, ff), BF16)] * 2,
        [
            pltpu.VMEM((experts, 2, width, ff), BF16),
            pltpu.VMEM((all_rows, width), BF16),
            pltpu.VMEM((all_rows, width), BF16),
            pltpu.VMEM((all_rows, width), F32),
            pltpu.VMEM((all_rows, width), F32),
            pltpu.VMEM((all_rows, LANES), F32),
            pltpu.VMEM((all_rows, LANES), F32),
            pltpu.SemaphoreType.DMA((sum(counts),)),
        ],
        20_000_000_000, 20_000_000, "expert_dgrad",
        [offs, router] + seconds + cots + [live] + flat_experts, len(flat_experts),
    )
    gs_parts = outs[:images]
    branch_parts = outs[images : 2 * images]
    dpre, hw = outs[2 * images :]
    gs_all = [gs_parts[0]] + [shift(gs_parts[j], "tensor", tensor, j) for j in range(1, tensor)]

    grads_in, grads_out = [], []
    vmem = pl.BlockSpec(memory_space=pltpu.VMEM)
    for e in range(experts):
        made = pl.pallas_call(
            functools.partial(expert_wgrad, blocks, n_out, rows, images),
            grid=(1,),
            out_shape=[jax.ShapeDtypeStruct((out_lead, 2, rows, ff), BF16)] * n_out,
            in_specs=[pl.BlockSpec(memory_space=pltpu.SMEM)]
            + [vmem] * (2 * images)
            + [pl.BlockSpec((1, all_rows, ff), functools.partial(lambda e, i: (e, 0, 0), e))] * 2,
            out_specs=[vmem] * n_out,
            scratch_shapes=[pltpu.VMEM((width, ff), F32)],
            compiler_params=pltpu.CompilerParams(vmem_limit_bytes=VMEM_LIMIT),
            cost_estimate=pl.CostEstimate(flops=4_000_000_000, bytes_accessed=8_000_000, transcendentals=0),
            name="expert_wgrad",
        )(offs, *seconds, *cots, dpre, hw)
        summed = reduce_dp(made[0], made[-1], dp)
        grads_in.append(summed[0])
        grads_out.append(summed[1].T)

    outs = call(
        functools.partial(
            attention_backward, attn_layout, rows, len(attn_arrays), blocks, n_out, images, experts, seq_len
        ),
        [jax.ShapeDtypeStruct((out_lead, 2 * groups, rows, 2 * cols), BF16)] * n_out
        + [jax.ShapeDtypeStruct((seq_len, width), F32), jax.ShapeDtypeStruct((8, width), F32)],
        [
            pltpu.VMEM((2 * groups, width, 2 * cols), BF16),
            pltpu.VMEM((width, 2 * cols), F32),
            pltpu.SemaphoreType.DMA((len(attn_arrays),)),
        ],
        16_000_000_000, 16_000_000, "attention_backward",
        [offs, tok, g1, g2, resid, second, first, qk, v, mixed, live[:seq], router, cot]
        + gs_all + attn_arrays,
        len(attn_arrays),
    )
    grad_tokens, small = outs[n_out:]

    tied = lax.optimization_barrier(tuple(branch_parts) + tuple(gs_all))[: len(branch_parts)]
    branch = tied[0].astype(F32)
    for j in range(1, tensor):
        branch = branch + shift(tied[j], "tensor", tensor, j).astype(F32)
    output = (resid + branch)[:seq_len].astype(BF16)

    part = reduce_dp(outs[0], outs[n_out - 1], dp)
    part_low = part.astype(BF16)
    total = part[:2]
    for j in range(1, tensor):
        total = total + shift(part_low[2 * j : 2 * j + 2], "tensor", tensor, j).astype(F32)
    grad_qkv = jnp.stack([total[0, :, :cols], total[0, :, cols:], total[1, :, :cols]])
    grad_out_weight = total[1, :, cols:].T

    if split:
        for axis, size, distance in (("tensor", 4, 1), ("tensor", 4, 2), ("dp", 8, 1), ("dp", 8, 2), ("dp", 8, 4)):
            small = small + shift(small, axis, size, distance)
    else:
        small = lax.psum(small, ("dp", "tensor"))
    return (
        output[None],
        grad_tokens[None],
        small[6],
        grad_qkv,
        grad_out_weight,
        small[7],
        small[:experts].T,
        jnp.stack(grads_in),
        jnp.stack(grads_out),
    )


def solution(mesh):
    sizes = dict(mesh.shape)
    return jax.shard_map(
        functools.partial(on_device, dp=sizes["dp"], tensor=sizes["tensor"]),
        mesh=mesh,
        in_specs=(
            P(("dp", "tensor"), None, None),
            P(),
            P(None, "dp", "tensor"),
            P("tensor", "dp"),
            P(),
            P(),
            P(None, "dp", "tensor"),
            P(None, "tensor", "dp"),
            P("dp", None, None),
            P("dp", None, None),
            P(("dp", "tensor"), None, None),
        ),
        out_specs=(
            P(("dp", "tensor"), None, None),
            P(("dp", "tensor"), None, None),
            P(),
            P(None, "dp", "tensor"),
            P("tensor", "dp"),
            P(),
            P(),
            P(None, "dp", "tensor"),
            P(None, "tensor", "dp"),
        ),
        check_vma=False,
    )
```

```python
import functools

import jax
import jax.numpy as jnp
from jax import lax
from jax.experimental import pallas as pl
from jax.experimental.pallas import tpu as pltpu
from jax.sharding import PartitionSpec as P

HD = 64
VALID = 197
CAP = 525
LANES = 128
EPSILON = 1e-06
NEGATIVE = -1e30
F32 = jnp.float32
BF16 = jnp.bfloat16
VMEM_LIMIT = 58 * 1024 * 1024

KEEP = (0, 2, 4, 6)
SEND = (1, 3, 5, 7)


def nn(a, b):
    return lax.dot_general(a, b, (((1,), (0,)), ((), ())), preferred_element_type=F32)


def nt(a, b):
    return lax.dot_general(a, b, (((1,), (1,)), ((), ())), preferred_element_type=F32)


def tn(a, b):
    return lax.dot_general(a, b, (((0,), (0,)), ((), ())), preferred_element_type=F32)


def norm_parts(values):
    centered = values - jnp.mean(values, axis=-1, keepdims=True)
    variance = jnp.mean(centered * centered, axis=-1, keepdims=True)
    inverse = lax.rsqrt(variance + EPSILON)
    return centered * inverse, inverse


def norm_backward(xhat, inverse, grad, gain):
    h = grad * gain
    mean_h = jnp.mean(h, axis=-1, keepdims=True)
    mean_hx = jnp.mean(h * xhat, axis=-1, keepdims=True)
    return inverse * (h - mean_h - xhat * mean_hx)


def shift(x, axis, size, distance):
    return lax.ppermute(x, axis, [(i, i ^ distance) for i in range(size)])


def after(x, *others):
    return lax.optimization_barrier((x,) + others)[0]


def near_dp(x, size):
    if size != 8:
        return ()
    return shift(x, "dp", size, 2), shift(x, "dp", size, 4)


def gather_dp(x, near, size, gate=(), core_gate=()):
    n = x.shape[0]
    if size != 8:
        full = lax.all_gather(x, "dp", axis=1, tiled=True)
        return [full], [(0, 0, 0, n, 0)], ()
    half = n // 2
    from_x, from_y = near
    low, high = from_x[:half], from_y[half:]
    if gate:
        low, high = lax.optimization_barrier((low, high) + tuple(gate))[:2]
    low = shift(low, "dp", size, 4)
    high = shift(high, "dp", size, 2)
    mine = jnp.concatenate([x, from_x, from_y, low, high])
    go = after(mine, *core_gate) if core_gate else mine
    spots = [(0, 0, n, 0), (n, 0, n, 2), (2 * n, 0, n, 4), (3 * n, 0, half, 6), (3 * n + half, half, n - half, 6)]
    layout = [(core,) + spot[:3] + (spot[3] ^ core,) for core in (0, 1) for spot in spots]
    return [mine, shift(go, "dp", size, 1)], layout, (low, high)


def reduce_dp(keep, send, size, small=None, gate=()):
    if size != 8:
        full = lax.psum_scatter(keep[0], "dp", scatter_dimension=1, tiled=True).astype(F32)
        return full, (), None if small is None else lax.psum(small, "dp"), ()
    n = keep.shape[1]
    half = n // 2

    def hop(x, distance):
        nonlocal small
        if small is None:
            return shift(x, "dp", size, distance)
        x, own, other = shift_with(x, small, "dp", size, distance)
        small = own + other
        return x

    if small is None:
        arrived = shift(send, "dp", size, 1)
    else:
        arrived, other = shift((send, small), "dp", size, 1)
        small = small + other
    total = [keep[j].astype(F32) + arrived[j].astype(F32) for j in range(4)]
    far = total[3].astype(BF16)
    low = hop(far[:half], 2).astype(F32)
    high = shift(far[half:], "dp", size, 4).astype(F32)
    to_x = jnp.concatenate([total[1][:half], total[1][half:] + high]).astype(BF16)
    to_y = jnp.concatenate([total[2][:half] + low, total[2][half:]]).astype(BF16)
    if gate:
        to_x, to_y = lax.optimization_barrier((to_x, to_y) + tuple(gate))[:2]
    from_x = shift(to_x, "dp", size, 2)
    from_y = hop(to_y, 4)
    return total[0] + from_x.astype(F32) + from_y.astype(F32), (to_x, to_y), small, (from_x, from_y)


def pack(small):
    coarse = small.astype(BF16)
    return jnp.concatenate([coarse, (small - coarse.astype(F32)).astype(BF16)])


def unpack(parts):
    count = parts.shape[0] // 2
    return parts[:count].astype(F32) + parts[count:].astype(F32)


def shift_with(x, small, axis, size, distance):
    lead = x.shape[0] * x.shape[1]
    parts = pack(small)
    sent = jnp.concatenate([x.reshape(lead, x.shape[2]), parts])
    got = shift(sent, axis, size, distance)
    return got[:lead].reshape(x.shape), unpack(parts), unpack(got[lead:])


def start_pieces(layout, refs, where, offs, rows, sems):
    copies = []
    for i, (array, src, lo, count, rel) in enumerate(layout):
        spot = pl.multiple_of(offs[rel], 16)
        copy = pltpu.make_async_copy(
            refs[array].at[pl.ds(src, count)], where.at[pl.ds(lo, count), pl.ds(spot, rows), :], sems.at[i]
        )
        copy.start()
        copies.append(copy)
    return copies


def attention_forward(layout, rows, count, offs, tokens, gain1, gain2, *rest):
    pieces = rest[:count]
    resid, second, first, qk_out, v_out, mixed_out, weights, sems = rest[count:]
    copies = start_pieces(layout, pieces, weights, offs, rows, sems)
    wide = tokens[...].astype(F32)
    xhat, _ = norm_parts(wide)
    fn = (xhat * gain1[...]).astype(BF16)
    first[...] = fn
    seq = fn.shape[0]
    for copy in copies:
        copy.wait()
    keys = lax.broadcasted_iota(jnp.int32, (seq, seq), 1) < VALID
    groups = weights.shape[0] // 2
    cols = weights.shape[2] // 2
    total = wide
    for g in range(groups):
        qk = nn(fn, weights[2 * g]).astype(BF16)
        v = nn(fn, weights[2 * g + 1])[:, :cols].astype(BF16)
        qk_out[g] = qk
        v_out[g] = v
        mixed = [jnp.zeros((seq, cols), BF16)]
        for h in range(cols // HD):
            q = qk[:, h * HD : (h + 1) * HD]
            k = qk[:, cols + h * HD : cols + (h + 1) * HD]
            s = jnp.where(keys, nt(q, k) * (HD**-0.5), NEGATIVE)
            e = jnp.exp(s - jnp.max(s, axis=-1, keepdims=True))
            p = e / jnp.sum(e, axis=-1, keepdims=True)
            mixed.append(nn(p.astype(BF16), v[:, h * HD : (h + 1) * HD]).astype(BF16))
        mixed = jnp.concatenate(mixed, axis=1)
        mixed_out[g] = mixed
        total = total + nt(mixed, weights[2 * g + 1])
    resid[...] = total
    xhat, _ = norm_parts(total)
    second[...] = (xhat * gain2[...]).astype(BF16)


def gate_softmax(second, router, experts):
    logits = nn(second, router)
    lane = lax.broadcasted_iota(jnp.int32, logits.shape, 1)
    logits = jnp.where(lane < experts, logits, NEGATIVE)
    e = jnp.exp(logits - jnp.max(logits, axis=-1, keepdims=True))
    return e / jnp.sum(e, axis=-1, keepdims=True)


def normal_cdf_pdf(x):
    z = jnp.abs(x) * 0.7071067811865476
    t = 1.0 / (1.0 + 0.3275911 * z)
    poly = t * (
        0.127414796
        + t * (-0.142248368 + t * (0.7107068705 + t * (-0.7265760135 + t * 0.5307027145)))
    )
    bell = jnp.exp(-0.5 * x * x)
    tail = poly * bell
    return jnp.where(x >= 0, 1.0 - tail, tail), bell * 0.3989422804014327


def put_blocks(acc, outs, blocks, index, offs, rows):
    for which, j, rel in blocks:
        spot = pl.multiple_of(offs[rel], 8)
        outs[which][(j,) + index] = acc[pl.ds(spot, rows), :].astype(BF16)


def expert_kernel(layout, rows, count, experts, images, parts, seq_len, blocks, n_out, offs, router, *rest):
    sn = rest[:images]
    cot = rest[images : images + images * parts]
    at = images + images * parts
    live = rest[at]
    pieces = rest[at + 1 : at + 1 + count]
    at += 1 + count
    earlier = None
    if blocks:
        earlier = rest[at]
        at += 1
    gs_out = rest[at : at + images]
    br_out = rest[at + images : at + 2 * images]
    outs = rest[at + 2 * images : at + 2 * images + n_out]
    weights, x_all, c_all, x_turned, c_turned, dpre_all, hw_all, acc, gs_acc, br_acc, w_acc, g_acc, *more = rest[
        at + 2 * images + n_out :
    ]
    if blocks:
        before, before_sems, sems = more
    else:
        (sems,) = more
    seq = sn[0].shape[0]
    copies = {}
    number = 0
    for e in range(experts):
        for i in (e, experts + e):
            for array, src, lo, n, rel in layout:
                if lo <= i < lo + n:
                    spot = pl.multiple_of(offs[rel], 16)
                    copy = pltpu.make_async_copy(
                        pieces[array].at[src + i - lo], weights.at[i, pl.ds(spot, rows), :], sems.at[number]
                    )
                    number += 1
                    copy.start()
                    copies.setdefault(e, []).append(copy)
    if blocks:
        older = [pltpu.make_async_copy(earlier.at[i], before.at[i], before_sems.at[i]) for i in range(2 * experts)]
        for copy in older:
            copy.start()
    for j in range(images):
        x_all[pl.ds(j * seq, seq), :] = sn[j][...]
        spot = j * seq
        for part in cot[j * parts : (j + 1) * parts]:
            c_all[pl.ds(spot, part.shape[0]), :] = part[...]
            spot += part.shape[0]
    x_turned[...] = x_all[...].T
    c_turned[...] = c_all[...].T
    for e in range(experts):
        for copy in copies[e]:
            copy.wait()

        def tile(j, carry):
            here = pl.ds(pl.multiple_of(j * seq, 16), seq)
            x = x_all[here, :]
            lane = lax.broadcasted_iota(jnp.int32, (seq, LANES), 1)
            if e == 0:
                w = gate_softmax(x, router[...], experts) * live[here, :].astype(F32)
                w_acc[here, :] = w
                g_prev = jnp.zeros((seq, LANES), F32)
            else:
                w = w_acc[here, :]
                g_prev = g_acc[here, :]
            we = w[:, e : e + 1]
            pre = nn(x, weights[e])
            gh = nn(c_all[here, :], weights[experts + e])
            cdf, pdf = normal_cdf_pdf(pre)
            hidden = (pre * cdf).astype(BF16).astype(F32)
            g = jnp.sum(hidden * gh, axis=-1, keepdims=True)
            hw = (hidden * we).astype(BF16)
            dpre = (gh * we * (cdf + pre * pdf)).astype(BF16)
            hw_all[here, :] = hw
            dpre_all[here, :] = dpre
            g_acc[here, :] = jnp.where((lane == e) | (lane == e + 4), g, g_prev)
            branch = nt(hw, weights[experts + e])
            gs = nt(dpre, weights[e])
            if e == 0:
                br_acc[here, :] = branch
                gs_acc[here, :] = gs
            else:
                br_acc[here, :] += branch
                gs_acc[here, :] += gs
            return carry

        lax.fori_loop(0, images, tile, 0)
        for i, left, right in ((e, x_turned, dpre_all), (experts + e, c_turned, hw_all)):
            total = nn(left[...], right[...])
            if blocks:
                older[i].wait()
                acc[...] = total + before[i].astype(F32)
                put_blocks(acc, outs, blocks, (i,), offs, rows)
            else:
                outs[0][i] = total.astype(BF16)
    for j in range(images):
        here = pl.ds(j * seq, seq)
        g = g_acc[here, :].T[:8, :]
        row = lax.broadcasted_iota(jnp.int32, g.shape, 0)
        coarse = g.astype(BF16).astype(F32)
        gs_acc[pl.ds(j * seq + seq_len, 8), 0:seq] = jnp.where(row < 4, coarse, g - coarse)
        gs_out[j][...] = gs_acc[here, :].astype(BF16)
        br_out[j][...] = br_acc[here, :].astype(BF16)


def attention_backward(
    layout, rows, count, blocks, n_out, images, experts, seq_len,
    offs, tokens, gain1, gain2, resid, second, first, qk_in, v_in, mixed_in, live, router, cot, *rest,
):
    gs_in = rest[:images]
    pieces = rest[images : images + count]
    at = images + count
    outs = rest[at : at + n_out]
    grad_tokens, small = rest[at + n_out : at + n_out + 2]
    weights, acc, sems = rest[at + n_out + 2 :]
    copies = start_pieces(layout, pieces, weights, offs, rows, sems)
    width = second.shape[1]
    seq = second.shape[0]
    gs = gs_in[0][...].astype(F32)
    for j in range(1, images):
        gs = gs + gs_in[j][...].astype(F32)
    shares = gs[seq_len : seq_len + 8, 0:seq]
    shares = jnp.concatenate([shares, jnp.zeros((LANES - 8, seq), F32)], axis=0).T
    shares = shares + jnp.concatenate([shares[:, 4:8], jnp.zeros((seq, LANES - 4), F32)], axis=1)
    lane = lax.broadcasted_iota(jnp.int32, shares.shape, 1)
    shares = jnp.where(lane < experts, shares, 0.0) * live[...].astype(F32)
    gs = jnp.where(lax.broadcasted_iota(jnp.int32, gs.shape, 0) < seq_len, gs, 0.0)
    sn = second[...]
    probs = gate_softmax(sn, router[...], experts)
    inner = jnp.sum(probs * shares, axis=-1, keepdims=True)
    grad_logits = (probs * (shares - inner)).astype(BF16)
    grad_router = tn(grad_logits, sn)[:8, :]
    gs = gs + nt(grad_logits, router[...])
    xhat, inverse = norm_parts(resid[...])
    gain2_row = jnp.sum(gs * xhat, axis=0, keepdims=True)
    grad_resid = cot[...].astype(F32) + norm_backward(xhat, inverse, gs, gain2[...])
    ga = grad_resid.astype(BF16)
    fn = first[...]
    keys = lax.broadcasted_iota(jnp.int32, (seq, seq), 1) < VALID
    scale = HD**-0.5
    groups = weights.shape[0] // 2
    cols = weights.shape[2] // 2
    for copy in copies:
        copy.wait()
    grad_first = None
    for g in range(groups):
        gm = nn(ga, weights[2 * g + 1])[:, cols:].astype(BF16)
        qk = qk_in[g]
        v = v_in[g]
        grads_q, grads_k, grads_v = [], [], []
        for h in range(cols // HD):
            q = qk[:, h * HD : (h + 1) * HD]
            k = qk[:, cols + h * HD : cols + (h + 1) * HD]
            gh = gm[:, h * HD : (h + 1) * HD]
            s = jnp.where(keys, nt(q, k) * scale, NEGATIVE)
            e = jnp.exp(s - jnp.max(s, axis=-1, keepdims=True))
            p = e / jnp.sum(e, axis=-1, keepdims=True)
            grads_v.append(tn(p.astype(BF16), gh).astype(BF16))
            gp = nt(gh, v[:, h * HD : (h + 1) * HD])
            ds = (p * (gp - jnp.sum(p * gp, axis=-1, keepdims=True))).astype(BF16)
            grads_q.append((nn(ds, k) * scale).astype(BF16))
            grads_k.append((tn(ds, q) * scale).astype(BF16))
        gqk = jnp.concatenate(grads_q + grads_k, axis=1)
        gv = jnp.concatenate(grads_v + [jnp.zeros((seq, cols), BF16)], axis=1)
        acc[...] = tn(fn, gqk)
        put_blocks(acc, outs, blocks, (2 * g,), offs, rows)
        acc[...] = tn(fn, gv) + tn(ga, mixed_in[g])
        put_blocks(acc, outs, blocks, (2 * g + 1,), offs, rows)
        part = nt(gqk, weights[2 * g]) + nt(gv, weights[2 * g + 1])
        grad_first = part if grad_first is None else grad_first + part
    xhat, inverse = norm_parts(tokens[...].astype(F32))
    gain1_row = jnp.sum(grad_first * xhat, axis=0, keepdims=True)
    result = grad_resid + norm_backward(xhat, inverse, grad_first, gain1[...])
    grad_tokens[...] = result[:seq_len]
    row = lax.broadcasted_iota(jnp.int32, (8, width), 0)
    found = jnp.where(row < experts, grad_router, jnp.where(row == 6, gain1_row, jnp.where(row == 7, gain2_row, 0.0)))
    small[...] = jnp.concatenate([found[:, i : i + small.shape[1]] for i in range(0, width, small.shape[1])], axis=0)


def call(kernel, out_shape, scratch, flops, n_bytes, name, operands, n_any, specs=None):
    total = len(operands)
    in_specs = [pl.BlockSpec(memory_space=pltpu.SMEM)]
    in_specs += [pl.BlockSpec(memory_space=pltpu.VMEM)] * (total - 1 - n_any)
    in_specs += [pl.BlockSpec(memory_space=pl.ANY)] * n_any
    if specs:
        for at, spec in specs.items():
            in_specs[at] = spec
    return pl.pallas_call(
        kernel,
        out_shape=out_shape,
        in_specs=in_specs,
        out_specs=jax.tree.map(lambda _: pl.BlockSpec(memory_space=pltpu.VMEM), out_shape),
        scratch_shapes=scratch,
        compiler_params=pltpu.CompilerParams(vmem_limit_bytes=VMEM_LIMIT),
        cost_estimate=pl.CostEstimate(flops=flops, bytes_accessed=n_bytes, transcendentals=0),
        name=name,
    )(*operands)


def on_device(
    tokens, gain_first, qkv_weight, out_weight, gain_second, router_weight,
    expert_in, expert_out, routes, slot_index, cotangent, *, dp, tensor,
):
    me = lax.axis_index("dp")
    z = lax.axis_index("tensor")
    _, seq_len, width = tokens.shape
    experts, own_rows, ff = expert_in.shape
    cols = qkv_weight.shape[2]
    seq = (seq_len + 8 + 15) // 16 * 16
    images = tensor
    split = dp == 8
    rel_count = 8 if split else 1
    rows = width // rel_count
    offs = ((me ^ jnp.arange(8, dtype=jnp.int32)) * rows) if split else jnp.zeros((8,), jnp.int32)
    offs = offs.astype(jnp.int32)
    blocks = (
        [(0, j, r) for j, r in enumerate(KEEP)] + [(1, j, r) for j, r in enumerate(SEND)]
        if split
        else [(0, 0, 0)]
    )
    n_out = 2 if split else 1
    out_lead = 4 if split else 1

    def pad_rows(x):
        return jnp.pad(x, ((0, seq - seq_len), (0, 0)))

    tok = pad_rows(tokens[0])
    cot = pad_rows(cotangent[0])
    g1 = gain_first.reshape(1, width)
    g2 = gain_second.reshape(1, width)
    router = jnp.pad(router_weight, ((0, 0), (0, LANES - experts)))

    own = jnp.stack(
        [
            jnp.concatenate([qkv_weight[0], qkv_weight[1]], axis=1),
            jnp.concatenate([qkv_weight[2], out_weight.T], axis=1),
        ]
    )
    z_pieces = [own] + [shift(own, "tensor", tensor, j) for j in range(1, tensor)]
    z_buffer = jnp.concatenate(z_pieces, axis=0)
    expert_own = jnp.concatenate([expert_in, jnp.swapaxes(expert_out, 1, 2)], axis=0)
    expert_near = near_dp(expert_own, dp)
    z_buffer = after(z_buffer, *expert_near)

    cut = seq // 32 * 16
    upper = after(cot[:cut], z_buffer)
    uppers = [shift(upper, "tensor", tensor, j) for j in range(1, tensor)]
    attn_arrays, attn_layout, attn_second = gather_dp(z_buffer, near_dp(z_buffer, dp), dp, uppers)
    lower = after(cot[cut:], *uppers)
    lowers = [shift(lower, "tensor", tensor, j) for j in range(1, tensor)]
    cots = [cot[:cut], cot[cut:]] + [part for pair in zip(uppers, lowers) for part in pair]
    groups = tensor
    resid, second, first, qk, v, mixed = call(
        functools.partial(attention_forward, attn_layout, rows, len(attn_arrays)),
        [
            jax.ShapeDtypeStruct((seq, width), F32),
            jax.ShapeDtypeStruct((seq, width), BF16),
            jax.ShapeDtypeStruct((seq, width), BF16),
            jax.ShapeDtypeStruct((groups, seq, 2 * cols), BF16),
            jax.ShapeDtypeStruct((groups, seq, cols), BF16),
            jax.ShapeDtypeStruct((groups, seq, 2 * cols), BF16),
        ],
        [
            pltpu.VMEM((2 * groups, width, 2 * cols), BF16),
            pltpu.SemaphoreType.DMA((len(attn_layout),)),
        ],
        8_000_000_000, 10_000_000, "attention_forward",
        [offs, tok, g1, g2] + attn_arrays, len(attn_arrays),
    )

    seconds = [second] + [shift(second, "tensor", tensor, j) for j in range(1, tensor)]
    live = (slot_index < CAP) & (jnp.arange(seq_len) < VALID)[None, :, None]
    expert_lane = jnp.arange(LANES)
    live = jnp.any((routes[..., None] == expert_lane) & live[..., None], axis=2).astype(BF16)
    live = jnp.pad(live, ((0, 0), (0, seq - seq_len), (0, 0)))
    live = jnp.concatenate([lax.dynamic_slice_in_dim(live, z ^ j, 1, 0)[0] for j in range(images)], axis=0)

    expert_arrays, expert_layout, _ = gather_dp(expert_own, expert_near, dp, attn_second, (second,))
    n_copies = sum(piece[3] for piece in expert_layout)

    def run_experts(first, count, earlier):
        rows_here = count * seq
        last = earlier is not None
        n_grads = n_out if last else 1
        grads = [jax.ShapeDtypeStruct((out_lead, 2 * experts, rows, ff), BF16)] * n_out
        whole = [jax.ShapeDtypeStruct((2 * experts, width, ff), BF16)]
        more = [pltpu.VMEM((2 * experts, width, ff), BF16), pltpu.SemaphoreType.DMA((2 * experts,))]
        return call(
            functools.partial(
                expert_kernel, expert_layout, rows, len(expert_arrays), experts, count, 2, seq_len,
                blocks if last else (), n_grads,
            ),
            [jax.ShapeDtypeStruct((seq, width), BF16)] * (2 * count) + (grads if last else whole),
            [
                pltpu.VMEM((2 * experts, width, ff), BF16),
                pltpu.VMEM((rows_here, width), BF16),
                pltpu.VMEM((rows_here, width), BF16),
                pltpu.VMEM((width, rows_here), BF16),
                pltpu.VMEM((width, rows_here), BF16),
                pltpu.VMEM((rows_here, ff), BF16),
                pltpu.VMEM((rows_here, ff), BF16),
                pltpu.VMEM((width, ff), F32),
                pltpu.VMEM((rows_here, width), F32),
                pltpu.VMEM((rows_here, width), F32),
                pltpu.VMEM((rows_here, LANES), F32),
                pltpu.VMEM((rows_here, LANES), F32),
            ]
            + (more if last else [])
            + [pltpu.SemaphoreType.DMA((n_copies,))],
            15_000_000_000, 20_000_000, "experts",
            [offs, router]
            + seconds[first : first + count]
            + cots[2 * first : 2 * (first + count)]
            + [live[first * seq : first * seq + rows_here]]
            + expert_arrays
            + ([earlier] if last else []),
            len(expert_arrays) + last,
        )

    near_images = images // 2
    outs = run_experts(0, near_images, None)
    gs_parts = list(outs[:near_images])
    branch_parts = list(outs[near_images : 2 * near_images])
    far_images = images - near_images
    outs = run_experts(near_images, far_images, outs[-1])
    gs_parts += outs[:far_images]
    branch_parts += outs[far_images : 2 * far_images]
    made = outs[2 * far_images :]
    gs_all = [gs_parts[0]] + [shift(gs_parts[j], "tensor", tensor, j) for j in range(1, tensor)]

    summed, on_way, _, near_sums = reduce_dp(made[0], made[-1], dp)
    grads_in = summed[:experts]
    grads_out = jnp.swapaxes(summed[experts:], 1, 2)
    if split:
        gs_all[0] = after(gs_all[0], *on_way)

    outs = call(
        functools.partial(
            attention_backward, attn_layout, rows, len(attn_arrays), blocks, n_out, images, experts, seq_len
        ),
        [jax.ShapeDtypeStruct((out_lead, 2 * groups, rows, 2 * cols), BF16)] * n_out
        + [jax.ShapeDtypeStruct((seq_len, width), F32), jax.ShapeDtypeStruct((8 * width // (2 * cols), 2 * cols), F32)],
        [
            pltpu.VMEM((2 * groups, width, 2 * cols), BF16),
            pltpu.VMEM((width, 2 * cols), F32),
            pltpu.SemaphoreType.DMA((len(attn_layout),)),
        ],
        16_000_000_000, 16_000_000, "attention_backward",
        [offs, tok, g1, g2, resid, second, first, qk, v, mixed, live[:seq], router, cot]
        + gs_all + attn_arrays,
        len(attn_arrays),
    )
    grad_tokens, small = outs[n_out:]

    tied = lax.optimization_barrier(tuple(branch_parts) + tuple(gs_all))[: len(branch_parts)]
    branches = [shift(tied[j], "tensor", tensor, j) for j in range(1, tensor)]
    branch = tied[0].astype(F32)
    for other in branches:
        branch = branch + other.astype(F32)
    output = (resid + branch)[:seq_len].astype(BF16)

    send = after(outs[n_out - 1], *branches[:-1], *near_sums)
    part, _, small, _ = reduce_dp(outs[0], send if split else None, dp, small, branches[-1:])
    part_low = part.astype(BF16)
    total = part[:2]
    smalls = []
    for j in range(1, tensor):
        block, mine, other = shift_with(part_low[2 * j : 2 * j + 2], small, "tensor", tensor, j)
        total = total + block.astype(F32)
        smalls = (smalls or [mine]) + [other]
    while len(smalls) > 1:
        smalls = [a + b for a, b in zip(smalls[::2], smalls[1::2])]
    small = jnp.concatenate([smalls[0][i : i + 8] for i in range(0, smalls[0].shape[0], 8)], axis=1)
    grad_qkv = jnp.stack([total[0, :, :cols], total[0, :, cols:], total[1, :, :cols]])
    grad_out_weight = total[1, :, cols:].T
    return (
        output[None],
        grad_tokens[None],
        small[6],
        grad_qkv,
        grad_out_weight,
        small[7],
        small[:experts].T,
        grads_in,
        grads_out,
    )


def solution(mesh):
    sizes = dict(mesh.shape)
    return jax.shard_map(
        functools.partial(on_device, dp=sizes["dp"], tensor=sizes["tensor"]),
        mesh=mesh,
        in_specs=(
            P(("dp", "tensor"), None, None),
            P(),
            P(None, "dp", "tensor"),
            P("tensor", "dp"),
            P(),
            P(),
            P(None, "dp", "tensor"),
            P(None, "tensor", "dp"),
            P("dp", None, None),
            P("dp", None, None),
            P(("dp", "tensor"), None, None),
        ),
        out_specs=(
            P(("dp", "tensor"), None, None),
            P(("dp", "tensor"), None, None),
            P(),
            P(None, "dp", "tensor"),
            P("tensor", "dp"),
            P(),
            P(),
            P(None, "dp", "tensor"),
            P(None, "tensor", "dp"),
        ),
        check_vma=False,
    )
```

```python
import functools

import jax
import jax.numpy as jnp
from jax import lax
from jax.experimental import pallas as pl
from jax.experimental.pallas import tpu as pltpu
from jax.sharding import PartitionSpec as P

HD = 64
VALID = 197
CAP = 525
LANES = 128
EPSILON = 1e-06
NEGATIVE = -1e30
F32 = jnp.float32
BF16 = jnp.bfloat16
VMEM_LIMIT = 58 * 1024 * 1024

KEEP = (0, 2, 4, 6)
SEND = (1, 3, 5, 7)


def nn(a, b):
    return lax.dot_general(a, b, (((1,), (0,)), ((), ())), preferred_element_type=F32)


def nt(a, b):
    return lax.dot_general(a, b, (((1,), (1,)), ((), ())), preferred_element_type=F32)


def tn(a, b):
    return lax.dot_general(a, b, (((0,), (0,)), ((), ())), preferred_element_type=F32)


def norm_parts(values):
    centered = values - jnp.mean(values, axis=-1, keepdims=True)
    variance = jnp.mean(centered * centered, axis=-1, keepdims=True)
    inverse = lax.rsqrt(variance + EPSILON)
    return centered * inverse, inverse


def norm_backward(xhat, inverse, grad, gain):
    h = grad * gain
    mean_h = jnp.mean(h, axis=-1, keepdims=True)
    mean_hx = jnp.mean(h * xhat, axis=-1, keepdims=True)
    return inverse * (h - mean_h - xhat * mean_hx)


def shift(x, axis, size, distance):
    return lax.ppermute(x, axis, [(i, i ^ distance) for i in range(size)])


def after(x, *others):
    return lax.optimization_barrier((x,) + others)[0]


def near_dp(x, size):
    if size != 8:
        return ()
    return shift(x, "dp", size, 2), shift(x, "dp", size, 4)


def gather_dp(x, near, size, gate=(), core_gate=None):
    n = x.shape[0]
    if size != 8:
        full = lax.all_gather(x, "dp", axis=1, tiled=True)
        return [full], [(0, 0, 0, n, 0)], ()
    half = n // 2
    from_x, from_y = near
    low, high = from_x[:half], from_y[half:]
    near_spots = [(0, 0, n, 0), (n, 0, n, 2), (2 * n, 0, n, 4)]
    far_spots = [(0, 0, half, 6), (half, half, n - half, 6)]
    arrays = []
    if core_gate is not None:
        mine = jnp.concatenate([x, from_x, from_y])
        arrays = [mine, shift(mine, "dp", size, 1)]
        gate = tuple(gate) + (arrays[1],)
    if gate:
        low, high = lax.optimization_barrier((low, high) + tuple(gate))[:2]
    low = shift(low, "dp", size, 4)
    high = shift(high, "dp", size, 2)
    if core_gate is not None:
        groups = [near_spots, far_spots]
        far = jnp.concatenate(lax.optimization_barrier((low, high) + tuple(core_gate))[:2])
        arrays += [far, shift(far, "dp", size, 1)]
    else:
        groups = [near_spots + [(3 * n + at, lo, count, rel) for at, lo, count, rel in far_spots]]
        mine = jnp.concatenate([x, from_x, from_y, low, high])
        arrays = [mine, shift(mine, "dp", size, 1)]
    layout = []
    for i, spots in enumerate(groups):
        for core in (0, 1):
            layout += [(2 * i + core, at, lo, count, rel ^ core) for at, lo, count, rel in spots]
    return arrays, layout, (low, high)


def reduce_dp(keep, send, size, small=None, gate=()):
    if size != 8:
        full = lax.psum_scatter(keep[0], "dp", scatter_dimension=1, tiled=True).astype(F32)
        return full, (), None if small is None else lax.psum(small, "dp"), ()
    n = keep.shape[1]
    half = n // 2

    def hop(x, distance):
        nonlocal small
        if small is None:
            return shift(x, "dp", size, distance)
        x, own, other = shift_with(x, small, "dp", size, distance)
        small = own + other
        return x

    if small is None:
        arrived = shift(send, "dp", size, 1)
    else:
        arrived, other = shift((send, small), "dp", size, 1)
        small = small + other
    total = [keep[j].astype(F32) + arrived[j].astype(F32) for j in range(4)]
    far = total[3].astype(BF16)
    low = hop(far[:half], 2).astype(F32)
    high = shift(far[half:], "dp", size, 4).astype(F32)
    to_x = jnp.concatenate([total[1][:half], total[1][half:] + high]).astype(BF16)
    to_y = jnp.concatenate([total[2][:half] + low, total[2][half:]]).astype(BF16)
    if gate:
        to_x, to_y = lax.optimization_barrier((to_x, to_y) + tuple(gate))[:2]
    from_x = shift(to_x, "dp", size, 2)
    from_y = hop(to_y, 4)
    return total[0] + from_x.astype(F32) + from_y.astype(F32), (to_x, to_y), small, (from_x, from_y)


def pack(small):
    coarse = small.astype(BF16)
    return jnp.concatenate([coarse, (small - coarse.astype(F32)).astype(BF16)])


def unpack(parts):
    count = parts.shape[0] // 2
    return parts[:count].astype(F32) + parts[count:].astype(F32)


def shift_with(x, small, axis, size, distance):
    lead = x.shape[0] * x.shape[1]
    parts = pack(small)
    sent = jnp.concatenate([x.reshape(lead, x.shape[2]), parts])
    got = shift(sent, axis, size, distance)
    return got[:lead].reshape(x.shape), unpack(parts), unpack(got[lead:])


def start_pieces(layout, refs, where, offs, rows, sems):
    copies = []
    for i, (array, src, lo, count, rel) in enumerate(layout):
        spot = pl.multiple_of(offs[rel], 16)
        copy = pltpu.make_async_copy(
            refs[array].at[pl.ds(src, count)], where.at[pl.ds(lo, count), pl.ds(spot, rows), :], sems.at[i]
        )
        copy.start()
        copies.append(copy)
    return copies


def attention_forward(layout, rows, count, offs, tokens, gain1, gain2, *rest):
    pieces = rest[:count]
    resid, second, first, qk_out, v_out, mixed_out, weights, sems = rest[count:]
    copies = start_pieces(layout, pieces, weights, offs, rows, sems)
    wide = tokens[...].astype(F32)
    xhat, _ = norm_parts(wide)
    fn = (xhat * gain1[...]).astype(BF16)
    first[...] = fn
    seq = fn.shape[0]
    for copy in copies:
        copy.wait()
    keys = lax.broadcasted_iota(jnp.int32, (seq, seq), 1) < VALID
    groups = weights.shape[0] // 2
    cols = weights.shape[2] // 2
    total = wide
    for g in range(groups):
        qk = nn(fn, weights[2 * g]).astype(BF16)
        v = nn(fn, weights[2 * g + 1])[:, :cols].astype(BF16)
        qk_out[g] = qk
        v_out[g] = v
        mixed = [jnp.zeros((seq, cols), BF16)]
        for h in range(cols // HD):
            q = qk[:, h * HD : (h + 1) * HD]
            k = qk[:, cols + h * HD : cols + (h + 1) * HD]
            s = jnp.where(keys, nt(q, k) * (HD**-0.5), NEGATIVE)
            e = jnp.exp(s - jnp.max(s, axis=-1, keepdims=True))
            p = e * (1.0 / jnp.sum(e, axis=-1, keepdims=True))
            mixed.append(nn(p.astype(BF16), v[:, h * HD : (h + 1) * HD]).astype(BF16))
        mixed = jnp.concatenate(mixed, axis=1)
        mixed_out[g] = mixed
        total = total + nt(mixed, weights[2 * g + 1])
    resid[...] = total
    xhat, _ = norm_parts(total)
    second[...] = (xhat * gain2[...]).astype(BF16)


def gate_softmax(second, router, experts):
    logits = nn(second, router)
    lane = lax.broadcasted_iota(jnp.int32, logits.shape, 1)
    logits = jnp.where(lane < experts, logits, NEGATIVE)
    e = jnp.exp(logits - jnp.max(logits, axis=-1, keepdims=True))
    return e / jnp.sum(e, axis=-1, keepdims=True)


def normal_cdf_pdf(x):
    return 0.5 + 0.5 * lax.erf(x * 0.5**0.5), jnp.exp(-0.5 * x * x) * 0.3989422804014327


def expert_kernel(layout, rows, count, experts, images, parts, seq_len, blocks, n_out, offs, router, *rest):
    sn = rest[:images]
    cot = rest[images : images + images * parts]
    at = images + images * parts
    live = rest[at]
    pieces = rest[at + 1 : at + 1 + count]
    at += 1 + count
    earlier = None
    if blocks:
        earlier = rest[at]
        at += 1
    gs_out = rest[at : at + images]
    br_out = rest[at + images : at + 2 * images]
    outs = rest[at + 2 * images : at + 2 * images + n_out]
    weights, x_all, c_all, x_turned, c_turned, dpre_all, hw_all, stage, gs_acc, br_acc, w_acc, g_acc, stage_sems, *more = rest[
        at + 2 * images + n_out :
    ]
    if blocks:
        before, before_sems, sems = more
    else:
        (sems,) = more
    seq = sn[0].shape[0]
    copies = {}
    number = 0
    for e in range(experts):
        for i in (e, experts + e):
            for array, src, lo, n, rel in layout:
                if lo <= i < lo + n:
                    spot = pl.multiple_of(offs[rel], 16)
                    copy = pltpu.make_async_copy(
                        pieces[array].at[src + i - lo], weights.at[i, pl.ds(spot, rows), :], sems.at[number]
                    )
                    number += 1
                    copy.start()
                    copies.setdefault(e, []).append(copy)
    if blocks:
        older = [pltpu.make_async_copy(earlier.at[i], before.at[i], before_sems.at[i]) for i in range(2 * experts)]
        for copy in older:
            copy.start()
    for j in range(images):
        x_all[pl.ds(j * seq, seq), :] = sn[j][...]
        spot = j * seq
        for part in cot[j * parts : (j + 1) * parts]:
            c_all[pl.ds(spot, part.shape[0]), :] = part[...]
            spot += part.shape[0]
    x_turned[...] = x_all[...].T
    c_turned[...] = c_all[...].T
    going = []
    for e in range(experts):
        for copy in copies[e]:
            copy.wait()
        x = x_all[...]
        if e == 0:
            w = gate_softmax(x, router[...], experts) * live[...].astype(F32)
            w_acc[...] = w
            g_prev = jnp.zeros(w.shape, F32)
        else:
            w = w_acc[...]
            g_prev = g_acc[...]
        we = w[:, e : e + 1]
        lane = lax.broadcasted_iota(jnp.int32, w.shape, 1)
        pre = nn(x, weights[e])
        gh = nn(c_all[...], weights[experts + e])
        cdf, pdf = normal_cdf_pdf(pre)
        hidden = (pre * cdf).astype(BF16).astype(F32)
        g = jnp.sum(hidden * gh, axis=-1, keepdims=True)
        hw = (hidden * we).astype(BF16)
        dpre = (gh * we * (cdf + pre * pdf)).astype(BF16)
        hw_all[...] = hw
        dpre_all[...] = dpre
        g_acc[...] = jnp.where((lane == e) | (lane == e + 4), g, g_prev)
        branch = nt(hw, weights[experts + e])
        gs = nt(dpre, weights[e])
        if e == 0:
            br_acc[...] = branch
            gs_acc[...] = gs
        else:
            br_acc[...] += branch
            gs_acc[...] += gs
        for i, left, right in ((e, x_turned, dpre_all), (experts + e, c_turned, hw_all)):
            total = nn(left[...], right[...])
            if blocks:
                older[i].wait()
                stage[i] = (total + before[i].astype(F32)).astype(BF16)
                for n, (which, j, rel) in enumerate(blocks):
                    spot = pl.multiple_of(offs[rel], 16)
                    going.append(
                        pltpu.make_async_copy(
                            stage.at[i, pl.ds(spot, rows), :], outs[which].at[j, i], stage_sems.at[i, n]
                        )
                    )
                    going[-1].start()
            else:
                stage[i] = total.astype(BF16)
                going.append(pltpu.make_async_copy(stage.at[i], outs[0].at[i], stage_sems.at[i, 0]))
                going[-1].start()
    for j in range(images):
        here = pl.ds(j * seq, seq)
        g = g_acc[here, :].T[:8, :]
        row = lax.broadcasted_iota(jnp.int32, g.shape, 0)
        coarse = g.astype(BF16).astype(F32)
        gs_acc[pl.ds(j * seq + seq_len, 8), 0:seq] = jnp.where(row < 4, coarse, g - coarse)
        gs_out[j][...] = gs_acc[here, :].astype(BF16)
        br_out[j][...] = br_acc[here, :].astype(BF16)
    for copy in going:
        copy.wait()


def attention_backward(
    layout, rows, count, blocks, n_out, images, experts, seq_len,
    offs, tokens, gain1, gain2, resid, second, first, qk_in, v_in, mixed_in, live, router, cot, *rest,
):
    gs_in = rest[:images]
    pieces = rest[images : images + count]
    at = images + count
    grad_tokens, small = rest[at : at + 2]
    at += 2
    outs = rest[at : at + n_out]
    weights, stage, stage_sems, sems = rest[at + n_out :]
    copies = start_pieces(layout, pieces, weights, offs, rows, sems)
    width = second.shape[1]
    seq = second.shape[0]
    gs = gs_in[0][...].astype(F32)
    for j in range(1, images):
        gs = gs + gs_in[j][...].astype(F32)
    shares = gs[seq_len : seq_len + 8, 0:seq]
    shares = jnp.concatenate([shares, jnp.zeros((LANES - 8, seq), F32)], axis=0).T
    shares = shares + jnp.concatenate([shares[:, 4:8], jnp.zeros((seq, LANES - 4), F32)], axis=1)
    lane = lax.broadcasted_iota(jnp.int32, shares.shape, 1)
    shares = jnp.where(lane < experts, shares, 0.0) * live[...].astype(F32)
    gs = jnp.where(lax.broadcasted_iota(jnp.int32, gs.shape, 0) < seq_len, gs, 0.0)
    sn = second[...]
    probs = gate_softmax(sn, router[...], experts)
    inner = jnp.sum(probs * shares, axis=-1, keepdims=True)
    grad_logits = (probs * (shares - inner)).astype(BF16)
    grad_router = tn(grad_logits, sn)[:8, :]
    gs = gs + nt(grad_logits, router[...])
    xhat, inverse = norm_parts(resid[...])
    gain2_row = jnp.sum(gs * xhat, axis=0, keepdims=True)
    grad_resid = cot[...].astype(F32) + norm_backward(xhat, inverse, gs, gain2[...])
    ga = grad_resid.astype(BF16)
    first_turned = first[...].T
    ga_turned = ga.T
    going = []

    def send_blocks(going, i):
        for n, (which, j, rel) in enumerate(blocks):
            spot = pl.multiple_of(offs[rel], 16)
            going.append(
                pltpu.make_async_copy(stage.at[i, pl.ds(spot, rows), :], outs[which].at[j, i], stage_sems.at[i, n])
            )
            going[-1].start()

    keys = lax.broadcasted_iota(jnp.int32, (seq, seq), 1) < VALID
    scale = HD**-0.5
    groups = weights.shape[0] // 2
    cols = weights.shape[2] // 2
    for copy in copies:
        copy.wait()
    grad_first = None
    for g in range(groups):
        gm = nn(ga, weights[2 * g + 1])[:, cols:].astype(BF16)
        qk = qk_in[g]
        v = v_in[g]
        grads_q, grads_k, grads_v = [], [], []
        for h in range(cols // HD):
            q = qk[:, h * HD : (h + 1) * HD]
            k = qk[:, cols + h * HD : cols + (h + 1) * HD]
            gh = gm[:, h * HD : (h + 1) * HD]
            s = jnp.where(keys, nt(q, k) * scale, NEGATIVE)
            e = jnp.exp(s - jnp.max(s, axis=-1, keepdims=True))
            p = e * (1.0 / jnp.sum(e, axis=-1, keepdims=True))
            grads_v.append(tn(p.astype(BF16), gh).astype(BF16))
            gp = nt(gh, v[:, h * HD : (h + 1) * HD])
            ds = (p * (gp - jnp.sum(p * gp, axis=-1, keepdims=True))).astype(BF16)
            grads_q.append((nn(ds, k) * scale).astype(BF16))
            grads_k.append((tn(ds, q) * scale).astype(BF16))
        gqk = jnp.concatenate(grads_q + grads_k, axis=1)
        gv = jnp.concatenate(grads_v + [jnp.zeros((seq, cols), BF16)], axis=1)
        stage[2 * g] = nn(first_turned, gqk).astype(BF16)
        send_blocks(going, 2 * g)
        stage[2 * g + 1] = (nn(first_turned, gv) + nn(ga_turned, mixed_in[g])).astype(BF16)
        send_blocks(going, 2 * g + 1)
        part = nt(gqk, weights[2 * g]) + nt(gv, weights[2 * g + 1])
        grad_first = part if grad_first is None else grad_first + part
    xhat, inverse = norm_parts(tokens[...].astype(F32))
    gain1_row = jnp.sum(grad_first * xhat, axis=0, keepdims=True)
    result = grad_resid + norm_backward(xhat, inverse, grad_first, gain1[...])
    grad_tokens[...] = result[:seq_len]
    row = lax.broadcasted_iota(jnp.int32, (8, width), 0)
    found = jnp.where(row < experts, grad_router, jnp.where(row == 6, gain1_row, jnp.where(row == 7, gain2_row, 0.0)))
    small[...] = jnp.concatenate([found[:, i : i + small.shape[1]] for i in range(0, width, small.shape[1])], axis=0)
    for copy in going:
        copy.wait()


def call(kernel, out_shape, scratch, flops, n_bytes, name, operands, n_any, n_any_out=0):
    total = len(operands)
    in_specs = [pl.BlockSpec(memory_space=pltpu.SMEM)]
    in_specs += [pl.BlockSpec(memory_space=pltpu.VMEM)] * (total - 1 - n_any)
    in_specs += [pl.BlockSpec(memory_space=pl.ANY)] * n_any
    out_specs = [pl.BlockSpec(memory_space=pltpu.VMEM)] * (len(out_shape) - n_any_out)
    out_specs += [pl.BlockSpec(memory_space=pl.ANY)] * n_any_out
    return pl.pallas_call(
        kernel,
        out_shape=out_shape,
        in_specs=in_specs,
        out_specs=out_specs,
        scratch_shapes=scratch,
        compiler_params=pltpu.CompilerParams(vmem_limit_bytes=VMEM_LIMIT),
        cost_estimate=pl.CostEstimate(flops=flops, bytes_accessed=n_bytes, transcendentals=0),
        name=name,
    )(*operands)


def call_experts(
    operands, layout, rows, n_arrays, experts, count, seq, seq_len, width, ff, blocks, n_out, out_lead
):
    last = bool(blocks)
    here = count * seq
    grads = [jax.ShapeDtypeStruct((out_lead, 2 * experts, rows, ff), BF16)] * n_out
    whole = [jax.ShapeDtypeStruct((2 * experts, width, ff), BF16)]
    more = [pltpu.VMEM((2 * experts, width, ff), BF16), pltpu.SemaphoreType.DMA((2 * experts,))]
    return call(
        functools.partial(
            expert_kernel, layout, rows, n_arrays, experts, count, 2, seq_len, blocks, n_out
        ),
        [jax.ShapeDtypeStruct((seq, width), BF16)] * (2 * count) + (grads if last else whole),
        [
            pltpu.VMEM((2 * experts, width, ff), BF16),
            pltpu.VMEM((here, width), BF16),
            pltpu.VMEM((here, width), BF16),
            pltpu.VMEM((width, here), BF16),
            pltpu.VMEM((width, here), BF16),
            pltpu.VMEM((here, ff), BF16),
            pltpu.VMEM((here, ff), BF16),
            pltpu.VMEM((2 * experts, width, ff), BF16),
            pltpu.VMEM((here, width), F32),
            pltpu.VMEM((here, width), F32),
            pltpu.VMEM((here, LANES), F32),
            pltpu.VMEM((here, LANES), F32),
            pltpu.SemaphoreType.DMA((2 * experts, max(1, len(blocks)))),
        ]
        + (more if last else [])
        + [pltpu.SemaphoreType.DMA((sum(piece[3] for piece in layout),))],
        15_000_000_000, 20_000_000, "experts", operands, n_arrays + last, n_any_out=len(grads if last else whole),
    )


def call_attention_forward(operands, layout, rows, n_arrays, seq, width, cols, groups):
    return call(
        functools.partial(attention_forward, layout, rows, n_arrays),
        [
            jax.ShapeDtypeStruct((seq, width), F32),
            jax.ShapeDtypeStruct((seq, width), BF16),
            jax.ShapeDtypeStruct((seq, width), BF16),
            jax.ShapeDtypeStruct((groups, seq, 2 * cols), BF16),
            jax.ShapeDtypeStruct((groups, seq, cols), BF16),
            jax.ShapeDtypeStruct((groups, seq, 2 * cols), BF16),
        ],
        [pltpu.VMEM((2 * groups, width, 2 * cols), BF16), pltpu.SemaphoreType.DMA((len(layout),))],
        8_000_000_000, 10_000_000, "attention_forward", operands, n_arrays,
    )


def call_attention_backward(
    operands, layout, rows, n_arrays, blocks, n_out, images, experts, seq_len, width, cols, groups, out_lead
):
    return call(
        functools.partial(
            attention_backward, layout, rows, n_arrays, blocks, n_out, images, experts, seq_len
        ),
        [jax.ShapeDtypeStruct((seq_len, width), F32), jax.ShapeDtypeStruct((8 * width // (2 * cols), 2 * cols), F32)]
        + [jax.ShapeDtypeStruct((out_lead, 2 * groups, rows, 2 * cols), BF16)] * n_out,
        [
            pltpu.VMEM((2 * groups, width, 2 * cols), BF16),
            pltpu.VMEM((2 * groups, width, 2 * cols), BF16),
            pltpu.SemaphoreType.DMA((2 * groups, len(blocks))),
            pltpu.SemaphoreType.DMA((len(layout),)),
        ],
        16_000_000_000, 16_000_000, "attention_backward", operands, n_arrays, n_any_out=n_out,
    )


def on_device(
    tokens, gain_first, qkv_weight, out_weight, gain_second, router_weight,
    expert_in, expert_out, routes, slot_index, cotangent, *, dp, tensor,
):
    me = lax.axis_index("dp")
    z = lax.axis_index("tensor")
    _, seq_len, width = tokens.shape
    experts, own_rows, ff = expert_in.shape
    cols = qkv_weight.shape[2]
    seq = (seq_len + 8 + 15) // 16 * 16
    images = tensor
    split = dp == 8
    rel_count = 8 if split else 1
    rows = width // rel_count
    offs = ((me ^ jnp.arange(8, dtype=jnp.int32)) * rows) if split else jnp.zeros((8,), jnp.int32)
    offs = offs.astype(jnp.int32)
    blocks = (
        [(0, j, r) for j, r in enumerate(KEEP)] + [(1, j, r) for j, r in enumerate(SEND)]
        if split
        else [(0, 0, 0)]
    )
    n_out = 2 if split else 1
    out_lead = 4 if split else 1

    def pad_rows(x):
        return jnp.pad(x, ((0, seq - seq_len), (0, 0)))

    tok = pad_rows(tokens[0])
    cot = pad_rows(cotangent[0])
    g1 = gain_first.reshape(1, width)
    g2 = gain_second.reshape(1, width)
    router = jnp.pad(router_weight, ((0, 0), (0, LANES - experts)))

    own = jnp.stack(
        [
            jnp.concatenate([qkv_weight[0], qkv_weight[1]], axis=1),
            jnp.concatenate([qkv_weight[2], out_weight.T], axis=1),
        ]
    )
    z_pieces = [own] + [shift(own, "tensor", tensor, j) for j in range(1, tensor)]
    z_buffer = jnp.concatenate(z_pieces, axis=0)
    expert_own = jnp.concatenate([expert_in, jnp.swapaxes(expert_out, 1, 2)], axis=0)
    expert_near = near_dp(expert_own, dp)
    z_buffer = after(z_buffer, *expert_near)

    cut = (seq // 32 + 1) * 16
    upper = after(cot[:cut], z_buffer)
    uppers = [shift(upper, "tensor", tensor, j) for j in range(1, tensor)]
    attn_arrays, attn_layout, attn_second = gather_dp(z_buffer, near_dp(z_buffer, dp), dp, uppers)
    lower = after(cot[cut:], *uppers)
    lowers = [shift(lower, "tensor", tensor, j) for j in range(1, tensor)]
    cots = [cot[:cut], cot[cut:]] + [part for pair in zip(uppers, lowers) for part in pair]
    groups = tensor
    resid, second, first, qk, v, mixed = call_attention_forward(
        [offs, tok, g1, g2] + attn_arrays, attn_layout, rows, len(attn_arrays), seq, width, cols, groups
    )

    seconds = [second] + [shift(second, "tensor", tensor, j) for j in range(1, tensor)]
    live = (slot_index < CAP) & (jnp.arange(seq_len) < VALID)[None, :, None]
    expert_lane = jnp.arange(LANES)
    live = jnp.any((routes[..., None] == expert_lane) & live[..., None], axis=2).astype(BF16)
    live = jnp.pad(live, ((0, 0), (0, seq - seq_len), (0, 0)))
    live = jnp.concatenate([lax.dynamic_slice_in_dim(live, z ^ j, 1, 0)[0] for j in range(images)], axis=0)

    expert_arrays, expert_layout, _ = gather_dp(expert_own, expert_near, dp, attn_second, (second, *lowers))
    def run_experts(first, count, earlier):
        operands = [offs, router] + seconds[first : first + count]
        operands += cots[2 * first : 2 * (first + count)]
        operands += [live[first * seq : (first + count) * seq]] + expert_arrays
        last = earlier is not None
        return call_experts(
            operands + ([earlier] if last else []), expert_layout, rows, len(expert_arrays),
            experts, count, seq, seq_len, width, ff, blocks if last else (), n_out if last else 1, out_lead,
        )

    near_images = images // 2
    outs = run_experts(0, near_images, None)
    gs_parts = list(outs[:near_images])
    branch_parts = list(outs[near_images : 2 * near_images])
    far_images = images - near_images
    outs = run_experts(near_images, far_images, outs[-1])
    gs_parts += outs[:far_images]
    branch_parts += outs[far_images : 2 * far_images]
    made = outs[2 * far_images :]
    gs_all = [gs_parts[0]] + [shift(gs_parts[j], "tensor", tensor, j) for j in range(1, tensor)]

    summed, on_way, _, near_sums = reduce_dp(made[0], made[-1], dp)
    grads_in = summed[:experts]
    grads_out = jnp.swapaxes(summed[experts:], 1, 2)
    if split:
        gs_all[0] = after(gs_all[0], *on_way)

    outs = call_attention_backward(
        [offs, tok, g1, g2, resid, second, first, qk, v, mixed, live[:seq], router, cot] + gs_all + attn_arrays,
        attn_layout, rows, len(attn_arrays), blocks, n_out, images, experts, seq_len, width, cols, groups, out_lead,
    )
    grad_tokens, small = outs[:2]
    outs = outs[2:]

    tied = lax.optimization_barrier(tuple(branch_parts) + tuple(gs_all))[: len(branch_parts)]
    branches = [shift(tied[j], "tensor", tensor, j) for j in range(1, tensor)]
    branch = tied[0].astype(F32)
    for other in branches:
        branch = branch + other.astype(F32)
    output = (resid + branch)[:seq_len].astype(BF16)

    send = after(outs[n_out - 1], *branches[:-1], *near_sums)
    part, _, small, _ = reduce_dp(outs[0], send if split else None, dp, small, branches[-1:])
    part_low = part.astype(BF16)
    total = part[:2]
    smalls = []
    for j in range(1, tensor):
        block, mine, other = shift_with(part_low[2 * j : 2 * j + 2], small, "tensor", tensor, j)
        total = total + block.astype(F32)
        smalls = (smalls or [mine]) + [other]
    while len(smalls) > 1:
        smalls = [a + b for a, b in zip(smalls[::2], smalls[1::2])]
    small = jnp.concatenate([smalls[0][i : i + 8] for i in range(0, smalls[0].shape[0], 8)], axis=1)
    grad_qkv = jnp.stack([total[0, :, :cols], total[0, :, cols:], total[1, :, :cols]])
    grad_out_weight = total[1, :, cols:].T
    return (
        output[None],
        grad_tokens[None],
        small[6],
        grad_qkv,
        grad_out_weight,
        small[7],
        small[:experts].T,
        grads_in,
        grads_out,
    )


def solution(mesh):
    sizes = dict(mesh.shape)
    return jax.shard_map(
        functools.partial(on_device, dp=sizes["dp"], tensor=sizes["tensor"]),
        mesh=mesh,
        in_specs=(
            P(("dp", "tensor"), None, None),
            P(),
            P(None, "dp", "tensor"),
            P("tensor", "dp"),
            P(),
            P(),
            P(None, "dp", "tensor"),
            P(None, "tensor", "dp"),
            P("dp", None, None),
            P("dp", None, None),
            P(("dp", "tensor"), None, None),
        ),
        out_specs=(
            P(("dp", "tensor"), None, None),
            P(("dp", "tensor"), None, None),
            P(),
            P(None, "dp", "tensor"),
            P("tensor", "dp"),
            P(),
            P(),
            P(None, "dp", "tensor"),
            P(None, "tensor", "dp"),
        ),
        check_vma=False,
    )
```

```python
import functools

import jax
import jax.numpy as jnp
from jax import lax
from jax.experimental import pallas as pl
from jax.experimental.pallas import tpu as pltpu
from jax.sharding import PartitionSpec as P

HD = 64
VALID = 197
CAP = 525
LANES = 128
EPSILON = 1e-06
NEGATIVE = -1e30
F32 = jnp.float32
BF16 = jnp.bfloat16
VMEM_LIMIT = 58 * 1024 * 1024

KEEP = (0, 2, 4, 6)
SEND = (1, 3, 5, 7)


def nn(a, b):
    return lax.dot_general(a, b, (((1,), (0,)), ((), ())), preferred_element_type=F32)


def nt(a, b):
    return lax.dot_general(a, b, (((1,), (1,)), ((), ())), preferred_element_type=F32)


def tn(a, b):
    return lax.dot_general(a, b, (((0,), (0,)), ((), ())), preferred_element_type=F32)


def norm_parts(values):
    centered = values - jnp.mean(values, axis=-1, keepdims=True)
    variance = jnp.mean(centered * centered, axis=-1, keepdims=True)
    inverse = lax.rsqrt(variance + EPSILON)
    return centered * inverse, inverse


def norm_backward(xhat, inverse, grad, gain):
    h = grad * gain
    mean_h = jnp.mean(h, axis=-1, keepdims=True)
    mean_hx = jnp.mean(h * xhat, axis=-1, keepdims=True)
    return inverse * (h - mean_h - xhat * mean_hx)


def shift(x, axis, size, distance):
    return lax.ppermute(x, axis, [(i, i ^ distance) for i in range(size)])


def after(x, *others):
    return lax.optimization_barrier((x,) + others)[0]


def join_kernel(count, *refs):
    parts, whole, sems = refs[:count], refs[count], refs[count + 1]
    at = 0
    copies = []
    for i, part in enumerate(parts):
        copies.append(pltpu.make_async_copy(part, whole.at[pl.ds(at, part.shape[0])], sems.at[i]))
        copies[-1].start()
        at += part.shape[0]
    for copy in copies:
        copy.wait()


def join(parts):
    lead = sum(part.shape[0] for part in parts)
    anywhere = pl.BlockSpec(memory_space=pl.ANY)
    return pl.pallas_call(
        functools.partial(join_kernel, len(parts)),
        out_shape=jax.ShapeDtypeStruct((lead,) + parts[0].shape[1:], parts[0].dtype),
        in_specs=[anywhere] * len(parts),
        out_specs=pl.BlockSpec(memory_space=pltpu.VMEM),
        scratch_shapes=[pltpu.SemaphoreType.DMA((len(parts),))],
        compiler_params=pltpu.CompilerParams(vmem_limit_bytes=VMEM_LIMIT),
        name="join",
    )(*parts)


def near_dp(x, size):
    if size != 8:
        return ()
    return shift(x, "dp", size, 2), shift(x, "dp", size, 4)


def gather_dp(x, near, size, gate=(), core_gate=None):
    n = x.shape[0]
    if size != 8:
        full = lax.all_gather(x, "dp", axis=1, tiled=True)
        return [full], [(0, 0, 0, n, 0)], ()
    half = n // 2
    from_x, from_y = near
    low, high = from_x[:half], from_y[half:]
    near_spots = [(0, 0, n, 0), (n, 0, n, 2), (2 * n, 0, n, 4)]
    far_spots = [(0, 0, half, 6), (half, half, n - half, 6)]
    arrays = []
    if core_gate is not None:
        mine = join([x, from_x, from_y])
        arrays = [mine, shift(mine, "dp", size, 1)]
        if core_gate:
            gate = tuple(gate) + (arrays[1],)
    if gate:
        low, high = lax.optimization_barrier((low, high) + tuple(gate))[:2]
    low = shift(low, "dp", size, 4)
    high = shift(high, "dp", size, 2)
    if core_gate is not None:
        groups = [near_spots, far_spots]
        far = join(lax.optimization_barrier((low, high) + tuple(core_gate))[:2])
        arrays += [far, shift(far, "dp", size, 1)]
    else:
        groups = [near_spots + [(3 * n + at, lo, count, rel) for at, lo, count, rel in far_spots]]
        mine = join([x, from_x, from_y, low, high])
        arrays = [mine, shift(mine, "dp", size, 1)]
    layout = []
    for i, spots in enumerate(groups):
        for core in (0, 1):
            layout += [(2 * i + core, at, lo, count, rel ^ core) for at, lo, count, rel in spots]
    return arrays, layout, (low, high)


def reduce_dp(keep, send, size, small=None, gate=()):
    if size != 8:
        full = lax.psum_scatter(sum(k[0] for k in keep), "dp", scatter_dimension=1, tiled=True).astype(F32)
        return full, (), None if small is None else lax.psum(small, "dp"), ()
    n = keep[0].shape[1]
    half = n // 2

    def hop(x, distance):
        nonlocal small
        if small is None:
            return shift(x, "dp", size, distance)
        x, own, other = shift_with(x, small, "dp", size, distance)
        small = own + other
        return x

    terms = keep + [shift(x, "dp", size, 1) for x in send]
    if small is not None:
        small = small + shift(small, "dp", size, 1)
    total = [sum(term[j].astype(F32) for term in terms) for j in range(4)]
    far = total[3].astype(BF16)
    low = hop(far[:half], 2).astype(F32)
    high = shift(far[half:], "dp", size, 4).astype(F32)
    to_x = jnp.concatenate([total[1][:half], total[1][half:] + high]).astype(BF16)
    to_y = jnp.concatenate([total[2][:half] + low, total[2][half:]]).astype(BF16)
    if gate:
        to_x, to_y = lax.optimization_barrier((to_x, to_y) + tuple(gate))[:2]
    from_x = shift(to_x, "dp", size, 2)
    from_y = hop(to_y, 4)
    return total[0] + from_x.astype(F32) + from_y.astype(F32), (to_x, to_y), small, (from_x, from_y)


def pack(small):
    coarse = small.astype(BF16)
    return jnp.concatenate([coarse, (small - coarse.astype(F32)).astype(BF16)])


def unpack(parts):
    count = parts.shape[0] // 2
    return parts[:count].astype(F32) + parts[count:].astype(F32)


def shift_with(x, small, axis, size, distance):
    lead = x.shape[0] * x.shape[1]
    parts = pack(small)
    sent = jnp.concatenate([x.reshape(lead, x.shape[2]), parts])
    got = shift(sent, axis, size, distance)
    return got[:lead].reshape(x.shape), unpack(parts), unpack(got[lead:])


def start_pieces(layout, refs, where, offs, rows, sems):
    copies = []
    for i, (array, src, lo, count, rel) in enumerate(layout):
        spot = pl.multiple_of(offs[rel], 16)
        copy = pltpu.make_async_copy(
            refs[array].at[pl.ds(src, count)], where.at[pl.ds(lo, count), pl.ds(spot, rows), :], sems.at[i]
        )
        copy.start()
        copies.append(copy)
    return copies


def attention_forward(layout, rows, count, offs, tokens, gain1, gain2, *rest):
    pieces = rest[:count]
    resid, second, first, qk_out, v_out, mixed_out, soft_out, weights, sems = rest[count:]
    copies = start_pieces(layout, pieces, weights, offs, rows, sems)
    wide = tokens[...].astype(F32)
    xhat, _ = norm_parts(wide)
    fn = (xhat * gain1[...]).astype(BF16)
    first[...] = fn
    seq = fn.shape[0]
    for copy in copies:
        copy.wait()
    keys = lax.broadcasted_iota(jnp.int32, (seq, seq), 1) < VALID
    groups = weights.shape[0] // 2
    cols = weights.shape[2] // 2
    total = wide
    for g in range(groups):
        qk = nn(fn, weights[2 * g]).astype(BF16)
        v = nn(fn, weights[2 * g + 1])[:, :cols].astype(BF16)
        qk_out[g] = qk
        v_out[g] = v
        mixed = [jnp.zeros((seq, cols), BF16)]
        for h in range(cols // HD):
            q = qk[:, h * HD : (h + 1) * HD]
            k = qk[:, cols + h * HD : cols + (h + 1) * HD]
            s = jnp.where(keys, nt(q, k) * (HD**-0.5), NEGATIVE)
            e = jnp.exp(s - jnp.max(s, axis=-1, keepdims=True))
            p = e * (1.0 / jnp.sum(e, axis=-1, keepdims=True))
            p = p.astype(BF16)
            soft_out[g * (cols // HD) + h] = p
            mixed.append(nn(p, v[:, h * HD : (h + 1) * HD]).astype(BF16))
        mixed = jnp.concatenate(mixed, axis=1)
        mixed_out[g] = mixed
        total = total + nt(mixed, weights[2 * g + 1])
    resid[...] = total
    xhat, _ = norm_parts(total)
    second[...] = (xhat * gain2[...]).astype(BF16)


def gate_softmax(second, router, experts):
    logits = nn(second, router)
    lane = lax.broadcasted_iota(jnp.int32, logits.shape, 1)
    logits = jnp.where(lane < experts, logits, NEGATIVE)
    e = jnp.exp(logits - jnp.max(logits, axis=-1, keepdims=True))
    return e / jnp.sum(e, axis=-1, keepdims=True)


def normal_cdf_pdf(x):
    return 0.5 + 0.5 * lax.erf(x * 0.5**0.5), jnp.exp(-0.5 * x * x) * 0.3989422804014327


def expert_kernel(layout, rows, count, experts, images, parts, seq_len, blocks, n_out, offs, router, *rest):
    sn = rest[:images]
    cot = rest[images : images + images * parts]
    at = images + images * parts
    live = rest[at]
    pieces = rest[at + 1 : at + 1 + count]
    at += 1 + count
    gs_out = rest[at : at + images]
    br_out = rest[at + images : at + 2 * images]
    outs = rest[at + 2 * images : at + 2 * images + n_out]
    weights, x_all, c_all, x_turned, c_turned, dpre_all, hw_all, stage, gs_acc, br_acc, w_acc, g_acc, stage_sems, sems = rest[
        at + 2 * images + n_out :
    ]
    seq = sn[0].shape[0]
    copies = {}
    number = 0
    for e in range(experts):
        for i in (e, experts + e):
            for array, src, lo, n, rel in layout:
                if lo <= i < lo + n:
                    spot = pl.multiple_of(offs[rel], 16)
                    copy = pltpu.make_async_copy(
                        pieces[array].at[src + i - lo], weights.at[i, pl.ds(spot, rows), :], sems.at[number]
                    )
                    number += 1
                    copy.start()
                    copies.setdefault(e, []).append(copy)
    for j in range(images):
        x_all[pl.ds(j * seq, seq), :] = sn[j][...]
        spot = j * seq
        for part in cot[j * parts : (j + 1) * parts]:
            c_all[pl.ds(spot, part.shape[0]), :] = part[...]
            spot += part.shape[0]
    x_turned[...] = x_all[...].T
    c_turned[...] = c_all[...].T
    going = []
    for e in range(experts):
        for copy in copies[e]:
            copy.wait()
        x = x_all[...]
        if e == 0:
            w = gate_softmax(x, router[...], experts) * live[...].astype(F32)
            w_acc[...] = w
            g_prev = jnp.zeros(w.shape, F32)
        else:
            w = w_acc[...]
            g_prev = g_acc[...]
        we = w[:, e : e + 1]
        lane = lax.broadcasted_iota(jnp.int32, w.shape, 1)
        pre = nn(x, weights[e])
        gh = nn(c_all[...], weights[experts + e])
        cdf, pdf = normal_cdf_pdf(pre)
        hidden = (pre * cdf).astype(BF16).astype(F32)
        g = jnp.sum(hidden * gh, axis=-1, keepdims=True)
        hw = (hidden * we).astype(BF16)
        dpre = (gh * we * (cdf + pre * pdf)).astype(BF16)
        hw_all[...] = hw
        dpre_all[...] = dpre
        g_acc[...] = jnp.where((lane == e) | (lane == e + 4), g, g_prev)
        branch = nt(hw, weights[experts + e])
        gs = nt(dpre, weights[e])
        if e == 0:
            br_acc[...] = branch
            gs_acc[...] = gs
        else:
            br_acc[...] += branch
            gs_acc[...] += gs
        for i, left, right in ((e, x_turned, dpre_all), (experts + e, c_turned, hw_all)):
            stage[i] = nn(left[...], right[...]).astype(BF16)
            for n, (which, j, rel) in enumerate(blocks):
                spot = pl.multiple_of(offs[rel], 16)
                going.append(
                    pltpu.make_async_copy(
                        stage.at[i, pl.ds(spot, rows), :], outs[which].at[j, i], stage_sems.at[i, n]
                    )
                )
                going[-1].start()
    for j in range(images):
        here = pl.ds(j * seq, seq)
        g = g_acc[here, :].T[:8, :]
        row = lax.broadcasted_iota(jnp.int32, g.shape, 0)
        coarse = g.astype(BF16).astype(F32)
        gs_acc[pl.ds(j * seq + seq_len, 8), 0:seq] = jnp.where(row < 4, coarse, g - coarse)
        gs_out[j][...] = gs_acc[here, :].astype(BF16)
        br_out[j][...] = br_acc[here, :].astype(BF16)
    for copy in going:
        copy.wait()


def attention_backward(
    layout, rows, count, blocks, n_out, images, experts, seq_len,
    offs, tokens, gain1, gain2, resid, second, first, qk_in, v_in, mixed_in, soft_in, live, router, cot, *rest,
):
    gs_in = rest[:images]
    pieces = rest[images : images + count]
    at = images + count
    grad_tokens, small = rest[at : at + 2]
    at += 2
    outs = rest[at : at + n_out]
    weights, stage, stage_sems, sems = rest[at + n_out :]
    copies = start_pieces(layout, pieces, weights, offs, rows, sems)
    width = second.shape[1]
    seq = second.shape[0]
    gs = gs_in[0][...].astype(F32)
    for j in range(1, images):
        gs = gs + gs_in[j][...].astype(F32)
    shares = gs[seq_len : seq_len + 8, 0:seq]
    shares = jnp.concatenate([shares, jnp.zeros((LANES - 8, seq), F32)], axis=0).T
    shares = shares + jnp.concatenate([shares[:, 4:8], jnp.zeros((seq, LANES - 4), F32)], axis=1)
    lane = lax.broadcasted_iota(jnp.int32, shares.shape, 1)
    shares = jnp.where(lane < experts, shares, 0.0) * live[...].astype(F32)
    gs = jnp.where(lax.broadcasted_iota(jnp.int32, gs.shape, 0) < seq_len, gs, 0.0)
    sn = second[...]
    probs = gate_softmax(sn, router[...], experts)
    inner = jnp.sum(probs * shares, axis=-1, keepdims=True)
    grad_logits = (probs * (shares - inner)).astype(BF16)
    grad_router = tn(grad_logits, sn)[:8, :]
    gs = gs + nt(grad_logits, router[...])
    xhat, inverse = norm_parts(resid[...])
    gain2_row = jnp.sum(gs * xhat, axis=0, keepdims=True)
    grad_resid = cot[...].astype(F32) + norm_backward(xhat, inverse, gs, gain2[...])
    ga = grad_resid.astype(BF16)
    first_turned = first[...].T
    ga_turned = ga.T
    going = []

    def send_blocks(going, i):
        for n, (which, j, rel) in enumerate(blocks):
            spot = pl.multiple_of(offs[rel], 16)
            going.append(
                pltpu.make_async_copy(stage.at[i, pl.ds(spot, rows), :], outs[which].at[j, i], stage_sems.at[i, n])
            )
            going[-1].start()

    scale = HD**-0.5
    groups = weights.shape[0] // 2
    cols = weights.shape[2] // 2
    for copy in copies:
        copy.wait()
    grad_first = None
    for g in range(groups):
        gm = nn(ga, weights[2 * g + 1])[:, cols:].astype(BF16)
        qk = qk_in[g]
        v = v_in[g]
        grads_q, grads_k, grads_v = [], [], []
        for h in range(cols // HD):
            q = qk[:, h * HD : (h + 1) * HD]
            k = qk[:, cols + h * HD : cols + (h + 1) * HD]
            gh = gm[:, h * HD : (h + 1) * HD]
            p = soft_in[g * (cols // HD) + h]
            grads_v.append(tn(p, gh).astype(BF16))
            p = p.astype(F32)
            gp = nt(gh, v[:, h * HD : (h + 1) * HD])
            ds = (p * (gp - jnp.sum(p * gp, axis=-1, keepdims=True))).astype(BF16)
            grads_q.append((nn(ds, k) * scale).astype(BF16))
            grads_k.append((tn(ds, q) * scale).astype(BF16))
        gqk = jnp.concatenate(grads_q + grads_k, axis=1)
        gv = jnp.concatenate(grads_v + [jnp.zeros((seq, cols), BF16)], axis=1)
        stage[2 * g] = nn(first_turned, gqk).astype(BF16)
        send_blocks(going, 2 * g)
        stage[2 * g + 1] = (nn(first_turned, gv) + nn(ga_turned, mixed_in[g])).astype(BF16)
        send_blocks(going, 2 * g + 1)
        part = nt(gqk, weights[2 * g]) + nt(gv, weights[2 * g + 1])
        grad_first = part if grad_first is None else grad_first + part
    xhat, inverse = norm_parts(tokens[...].astype(F32))
    gain1_row = jnp.sum(grad_first * xhat, axis=0, keepdims=True)
    result = grad_resid + norm_backward(xhat, inverse, grad_first, gain1[...])
    grad_tokens[...] = result[:seq_len]
    row = lax.broadcasted_iota(jnp.int32, (8, width), 0)
    found = jnp.where(row < experts, grad_router, jnp.where(row == 6, gain1_row, jnp.where(row == 7, gain2_row, 0.0)))
    small[...] = jnp.concatenate([found[:, i : i + small.shape[1]] for i in range(0, width, small.shape[1])], axis=0)
    for copy in going:
        copy.wait()


def call(kernel, out_shape, scratch, flops, n_bytes, name, operands, n_any, n_any_out=0):
    total = len(operands)
    in_specs = [pl.BlockSpec(memory_space=pltpu.SMEM)]
    in_specs += [pl.BlockSpec(memory_space=pltpu.VMEM)] * (total - 1 - n_any)
    in_specs += [pl.BlockSpec(memory_space=pl.ANY)] * n_any
    out_specs = [pl.BlockSpec(memory_space=pltpu.VMEM)] * (len(out_shape) - n_any_out)
    out_specs += [pl.BlockSpec(memory_space=pl.ANY)] * n_any_out
    return pl.pallas_call(
        kernel,
        out_shape=out_shape,
        in_specs=in_specs,
        out_specs=out_specs,
        scratch_shapes=scratch,
        compiler_params=pltpu.CompilerParams(vmem_limit_bytes=VMEM_LIMIT),
        cost_estimate=pl.CostEstimate(flops=flops, bytes_accessed=n_bytes, transcendentals=0),
        name=name,
    )(*operands)


def call_experts(
    operands, layout, rows, n_arrays, experts, count, parts, seq, seq_len, width, ff, blocks, n_out, out_lead
):
    here = count * seq
    grads = [jax.ShapeDtypeStruct((out_lead, 2 * experts, rows, ff), BF16)] * n_out
    return call(
        functools.partial(
            expert_kernel, layout, rows, n_arrays, experts, count, parts, seq_len, blocks, n_out
        ),
        [jax.ShapeDtypeStruct((seq, width), BF16)] * (2 * count) + grads,
        [
            pltpu.VMEM((2 * experts, width, ff), BF16),
            pltpu.VMEM((here, width), BF16),
            pltpu.VMEM((here, width), BF16),
            pltpu.VMEM((width, here), BF16),
            pltpu.VMEM((width, here), BF16),
            pltpu.VMEM((here, ff), BF16),
            pltpu.VMEM((here, ff), BF16),
            pltpu.VMEM((2 * experts, width, ff), BF16),
            pltpu.VMEM((here, width), F32),
            pltpu.VMEM((here, width), F32),
            pltpu.VMEM((here, LANES), F32),
            pltpu.VMEM((here, LANES), F32),
            pltpu.SemaphoreType.DMA((2 * experts, len(blocks))),
            pltpu.SemaphoreType.DMA((sum(piece[3] for piece in layout),)),
        ],
        15_000_000_000, 20_000_000, "experts", operands, n_arrays, n_any_out=n_out,
    )


def call_attention_forward(operands, layout, rows, n_arrays, seq, width, cols, groups):
    return call(
        functools.partial(attention_forward, layout, rows, n_arrays),
        [
            jax.ShapeDtypeStruct((seq, width), F32),
            jax.ShapeDtypeStruct((seq, width), BF16),
            jax.ShapeDtypeStruct((seq, width), BF16),
            jax.ShapeDtypeStruct((groups, seq, 2 * cols), BF16),
            jax.ShapeDtypeStruct((groups, seq, cols), BF16),
            jax.ShapeDtypeStruct((groups, seq, 2 * cols), BF16),
            jax.ShapeDtypeStruct((groups * cols // HD, seq, seq), BF16),
        ],
        [pltpu.VMEM((2 * groups, width, 2 * cols), BF16), pltpu.SemaphoreType.DMA((len(layout),))],
        8_000_000_000, 10_000_000, "attention_forward", operands, n_arrays,
    )


def call_attention_backward(
    operands, layout, rows, n_arrays, blocks, n_out, images, experts, seq_len, width, cols, groups, out_lead
):
    return call(
        functools.partial(
            attention_backward, layout, rows, n_arrays, blocks, n_out, images, experts, seq_len
        ),
        [jax.ShapeDtypeStruct((seq_len, width), F32), jax.ShapeDtypeStruct((8 * width // (2 * cols), 2 * cols), F32)]
        + [jax.ShapeDtypeStruct((out_lead, 2 * groups, rows, 2 * cols), BF16)] * n_out,
        [
            pltpu.VMEM((2 * groups, width, 2 * cols), BF16),
            pltpu.VMEM((2 * groups, width, 2 * cols), BF16),
            pltpu.SemaphoreType.DMA((2 * groups, len(blocks))),
            pltpu.SemaphoreType.DMA((len(layout),)),
        ],
        16_000_000_000, 16_000_000, "attention_backward", operands, n_arrays, n_any_out=n_out,
    )


def on_device(
    tokens, gain_first, qkv_weight, out_weight, gain_second, router_weight,
    expert_in, expert_out, routes, slot_index, cotangent, *, dp, tensor,
):
    me = lax.axis_index("dp")
    z = lax.axis_index("tensor")
    _, seq_len, width = tokens.shape
    experts, own_rows, ff = expert_in.shape
    cols = qkv_weight.shape[2]
    seq = (seq_len + 8 + 15) // 16 * 16
    images = tensor
    split = dp == 8
    rel_count = 8 if split else 1
    rows = width // rel_count
    offs = ((me ^ jnp.arange(8, dtype=jnp.int32)) * rows) if split else jnp.zeros((8,), jnp.int32)
    offs = offs.astype(jnp.int32)
    blocks = (
        [(0, j, r) for j, r in enumerate(KEEP)] + [(1, j, r) for j, r in enumerate(SEND)]
        if split
        else [(0, 0, 0)]
    )
    n_out = 2 if split else 1
    out_lead = 4 if split else 1

    def pad_rows(x):
        return jnp.pad(x, ((0, seq - seq_len), (0, 0)))

    tok = pad_rows(tokens[0])
    cot = pad_rows(cotangent[0])
    g1 = gain_first.reshape(1, width)
    g2 = gain_second.reshape(1, width)
    router = jnp.pad(router_weight, ((0, 0), (0, LANES - experts)))

    own = jnp.stack(
        [
            jnp.concatenate([qkv_weight[0], qkv_weight[1]], axis=1),
            jnp.concatenate([qkv_weight[2], out_weight.T], axis=1),
        ]
    )
    z_pieces = [own] + [shift(own, "tensor", tensor, j) for j in range(1, tensor)]
    z_buffer = jnp.concatenate(z_pieces, axis=0)
    expert_own = jnp.concatenate([expert_in, jnp.swapaxes(expert_out, 1, 2)], axis=0)
    expert_near = near_dp(expert_own, dp)
    z_buffer = after(z_buffer, *expert_near)

    near_images = images // 2
    cot_go = after(cot, z_buffer)
    straight = [shift(cot_go, "tensor", tensor, j) for j in range(1, near_images + 1)]
    attn_arrays, attn_layout, attn_second = gather_dp(z_buffer, near_dp(z_buffer, dp), dp, straight)
    relayed = [shift(straight[-1], "tensor", tensor, j) for j in range(1, images - near_images)]
    cots = [[cot] + straight[:-1], straight[-1:] + relayed]

    groups = tensor
    resid, second, first, qk, v, mixed, soft = call_attention_forward(
        [offs, tok, g1, g2] + attn_arrays, attn_layout, rows, len(attn_arrays), seq, width, cols, groups
    )

    seconds = [second] + [shift(second, "tensor", tensor, j) for j in range(1, tensor)]
    live = (slot_index < CAP) & (jnp.arange(seq_len) < VALID)[None, :, None]
    expert_lane = jnp.arange(LANES)
    live = jnp.any((routes[..., None] == expert_lane) & live[..., None], axis=2).astype(BF16)
    live = jnp.pad(live, ((0, 0), (0, seq - seq_len), (0, 0)))
    live = jnp.concatenate([lax.dynamic_slice_in_dim(live, z ^ j, 1, 0)[0] for j in range(images)], axis=0)

    expert_arrays, expert_layout, _ = gather_dp(expert_own, expert_near, dp, attn_second, (second, *relayed))
    gs_parts, branch_parts, made = [], [], []
    for (begin, count), cot_parts in zip(((0, near_images), (near_images, images - near_images)), cots):
        outs = call_experts(
            [offs, router]
            + seconds[begin : begin + count]
            + cot_parts
            + [after(live[begin * seq : (begin + count) * seq], *gs_parts)]
            + expert_arrays,
            expert_layout, rows, len(expert_arrays), experts, count, len(cot_parts) // count, seq, seq_len, width, ff, blocks, n_out, out_lead,
        )
        gs_parts += outs[:count]
        branch_parts += outs[count : 2 * count]
        made.append(outs[2 * count :])
    gs_all = [gs_parts[0]] + [shift(gs_parts[j], "tensor", tensor, j) for j in range(1, tensor)]

    summed, on_way, _, near_sums = reduce_dp([m[0] for m in made], [m[-1] for m in made], dp)
    grads_in = summed[:experts]
    grads_out = jnp.swapaxes(summed[experts:], 1, 2)
    if split:
        gs_all[0] = after(gs_all[0], *on_way)

    outs = call_attention_backward(
        [offs, tok, g1, g2, resid, second, first, qk, v, mixed, soft, live[:seq], router, cot] + gs_all + attn_arrays,
        attn_layout, rows, len(attn_arrays), blocks, n_out, images, experts, seq_len, width, cols, groups, out_lead,
    )
    grad_tokens, small = outs[:2]
    outs = outs[2:]

    tied = lax.optimization_barrier(tuple(branch_parts) + tuple(gs_all))[: len(branch_parts)]
    branches = [shift(tied[j], "tensor", tensor, j) for j in range(1, tensor)]
    branch = tied[0].astype(F32)
    for other in branches:
        branch = branch + other.astype(F32)
    output = (resid + branch)[:seq_len].astype(BF16)

    send = after(outs[n_out - 1], *branches[:-1], *near_sums)
    part, _, small, _ = reduce_dp([outs[0]], [send], dp, small, branches[-1:])
    part_low = part.astype(BF16)
    total = part[:2]
    smalls = []
    for j in range(1, tensor):
        block, mine, other = shift_with(part_low[2 * j : 2 * j + 2], small, "tensor", tensor, j)
        total = total + block.astype(F32)
        smalls = (smalls or [mine]) + [other]
    while len(smalls) > 1:
        smalls = [a + b for a, b in zip(smalls[::2], smalls[1::2])]
    small = jnp.concatenate([smalls[0][i : i + 8] for i in range(0, smalls[0].shape[0], 8)], axis=1)
    grad_qkv = jnp.stack([total[0, :, :cols], total[0, :, cols:], total[1, :, :cols]])
    grad_out_weight = total[1, :, cols:].T
    return (
        output[None],
        grad_tokens[None],
        small[6],
        grad_qkv,
        grad_out_weight,
        small[7],
        small[:experts].T,
        grads_in,
        grads_out,
    )


def solution(mesh):
    sizes = dict(mesh.shape)
    return jax.shard_map(
        functools.partial(on_device, dp=sizes["dp"], tensor=sizes["tensor"]),
        mesh=mesh,
        in_specs=(
            P(("dp", "tensor"), None, None),
            P(),
            P(None, "dp", "tensor"),
            P("tensor", "dp"),
            P(),
            P(),
            P(None, "dp", "tensor"),
            P(None, "tensor", "dp"),
            P("dp", None, None),
            P("dp", None, None),
            P(("dp", "tensor"), None, None),
        ),
        out_specs=(
            P(("dp", "tensor"), None, None),
            P(("dp", "tensor"), None, None),
            P(),
            P(None, "dp", "tensor"),
            P("tensor", "dp"),
            P(),
            P(),
            P(None, "dp", "tensor"),
            P(None, "tensor", "dp"),
        ),
        check_vma=False,
    )
```

```python
import functools

import jax
import jax.numpy as jnp
from jax import lax
from jax.experimental import pallas as pl
from jax.experimental.pallas import tpu as pltpu
from jax.sharding import PartitionSpec as P

HD = 64
VALID = 197
CAP = 525
LANES = 128
EPSILON = 1e-06
NEGATIVE = -1e30
F32 = jnp.float32
BF16 = jnp.bfloat16
VMEM_LIMIT = 58 * 1024 * 1024

KEEP = (0, 2, 4, 6)
SEND = (1, 3, 5, 7)


def nn(a, b):
    return lax.dot_general(a, b, (((1,), (0,)), ((), ())), preferred_element_type=F32)


def nt(a, b):
    return lax.dot_general(a, b, (((1,), (1,)), ((), ())), preferred_element_type=F32)


def tn(a, b):
    return lax.dot_general(a, b, (((0,), (0,)), ((), ())), preferred_element_type=F32)


def norm_parts(values):
    centered = values - jnp.mean(values, axis=-1, keepdims=True)
    variance = jnp.mean(centered * centered, axis=-1, keepdims=True)
    inverse = lax.rsqrt(variance + EPSILON)
    return centered * inverse, inverse


def norm_backward(xhat, inverse, grad, gain):
    h = grad * gain
    mean_h = jnp.mean(h, axis=-1, keepdims=True)
    mean_hx = jnp.mean(h * xhat, axis=-1, keepdims=True)
    return inverse * (h - mean_h - xhat * mean_hx)


def shift(x, axis, size, distance):
    return lax.ppermute(x, axis, [(i, i ^ distance) for i in range(size)])


def after(x, *others):
    return lax.optimization_barrier((x,) + others)[0]


def join_kernel(count, *refs):
    parts, whole, sems = refs[:count], refs[count], refs[count + 1]
    at = 0
    copies = []
    for i, part in enumerate(parts):
        copies.append(pltpu.make_async_copy(part, whole.at[pl.ds(at, part.shape[0])], sems.at[i]))
        copies[-1].start()
        at += part.shape[0]
    for copy in copies:
        copy.wait()


def join(parts):
    lead = sum(part.shape[0] for part in parts)
    anywhere = pl.BlockSpec(memory_space=pl.ANY)
    return pl.pallas_call(
        functools.partial(join_kernel, len(parts)),
        out_shape=jax.ShapeDtypeStruct((lead,) + parts[0].shape[1:], parts[0].dtype),
        in_specs=[anywhere] * len(parts),
        out_specs=pl.BlockSpec(memory_space=pltpu.VMEM),
        scratch_shapes=[pltpu.SemaphoreType.DMA((len(parts),))],
        compiler_params=pltpu.CompilerParams(vmem_limit_bytes=VMEM_LIMIT),
        name="join",
    )(*parts)


def near_dp(x, size):
    if size != 8:
        return ()
    return shift(x, "dp", size, 2), shift(x, "dp", size, 4)


def gather_dp(x, near, size, gate=(), core_gate=None):
    n = x.shape[0]
    if size != 8:
        full = lax.all_gather(x, "dp", axis=1, tiled=True)
        return [full], [(0, 0, 0, n, 0)], ()
    half = n // 2
    from_x, from_y = near
    low, high = from_x[:half], from_y[half:]
    near_spots = [(0, 0, n, 0), (n, 0, n, 2), (2 * n, 0, n, 4)]
    far_spots = [(0, 0, half, 6), (half, half, n - half, 6)]
    arrays = []
    if core_gate is not None:
        mine = join([x, from_x, from_y])
        arrays = [mine, shift(mine, "dp", size, 1)]
        if core_gate:
            gate = tuple(gate) + (arrays[1],)
    if gate:
        low, high = lax.optimization_barrier((low, high) + tuple(gate))[:2]
    low = shift(low, "dp", size, 4)
    high = shift(high, "dp", size, 2)
    if core_gate is not None:
        groups = [near_spots, [(0, 0, half, 6)], [(0, half, n - half, 6)]]
        for far in lax.optimization_barrier((low, high) + tuple(core_gate))[:2]:
            arrays += [far, shift(far, "dp", size, 1)]
    else:
        groups = [near_spots + [(3 * n + at, lo, count, rel) for at, lo, count, rel in far_spots]]
        mine = join([x, from_x, from_y, low, high])
        arrays = [mine, shift(mine, "dp", size, 1)]
    layout = []
    for i, spots in enumerate(groups):
        for core in (0, 1):
            layout += [(2 * i + core, at, lo, count, rel ^ core) for at, lo, count, rel in spots]
    return arrays, layout, (low, high)


def reduce_dp(keep, send, size, small=None, gate=()):
    if size != 8:
        full = lax.psum_scatter(sum(k[0] for k in keep), "dp", scatter_dimension=1, tiled=True).astype(F32)
        return full, (), None if small is None else lax.psum(small, "dp"), ()
    n = keep[0].shape[1]
    half = n // 2

    def hop(x, distance):
        nonlocal small
        if small is None:
            return shift(x, "dp", size, distance)
        x, own, other = shift_with(x, small, "dp", size, distance)
        small = own + other
        return x

    terms = keep + [shift(x, "dp", size, 1) for x in send]
    if small is not None:
        small = small + shift(small, "dp", size, 1)
    total = [sum(term[j].astype(F32) for term in terms) for j in range(4)]
    far = total[3].astype(BF16)
    low = hop(far[:half], 2).astype(F32)
    high = shift(far[half:], "dp", size, 4).astype(F32)
    to_x = jnp.concatenate([total[1][:half], total[1][half:] + high]).astype(BF16)
    to_y = jnp.concatenate([total[2][:half] + low, total[2][half:]]).astype(BF16)
    if gate:
        to_x, to_y = lax.optimization_barrier((to_x, to_y) + tuple(gate))[:2]
    from_x = shift(to_x, "dp", size, 2)
    from_y = hop(to_y, 4)
    return total[0] + from_x.astype(F32) + from_y.astype(F32), (to_x, to_y), small, (from_x, from_y)


def pack(small):
    coarse = small.astype(BF16)
    return jnp.concatenate([coarse, (small - coarse.astype(F32)).astype(BF16)])


def unpack(parts):
    count = parts.shape[0] // 2
    return parts[:count].astype(F32) + parts[count:].astype(F32)


def shift_with(x, small, axis, size, distance):
    lead = x.shape[0] * x.shape[1]
    parts = pack(small)
    sent = jnp.concatenate([x.reshape(lead, x.shape[2]), parts])
    got = shift(sent, axis, size, distance)
    return got[:lead].reshape(x.shape), unpack(parts), unpack(got[lead:])


def start_pieces(layout, refs, where, offs, rows, sems):
    copies = []
    for i, (array, src, lo, count, rel) in enumerate(layout):
        spot = pl.multiple_of(offs[rel], 16)
        copy = pltpu.make_async_copy(
            refs[array].at[pl.ds(src, count)], where.at[pl.ds(lo, count), pl.ds(spot, rows), :], sems.at[i]
        )
        copy.start()
        copies.append(copy)
    return copies


def attention_forward(layout, rows, count, offs, tokens, gain1, gain2, *rest):
    pieces = rest[:count]
    resid, second, first, qk_out, v_out, mixed_out, soft_out, weights, sems = rest[count:]
    copies = start_pieces(layout, pieces, weights, offs, rows, sems)
    wide = tokens[...].astype(F32)
    xhat, _ = norm_parts(wide)
    fn = (xhat * gain1[...]).astype(BF16)
    first[...] = fn
    seq = fn.shape[0]
    for copy in copies:
        copy.wait()
    keys = lax.broadcasted_iota(jnp.int32, (seq, seq), 1) < VALID
    groups = weights.shape[0] // 2
    cols = weights.shape[2] // 2
    total = wide
    for g in range(groups):
        qk = nn(fn, weights[2 * g]).astype(BF16)
        v = nn(fn, weights[2 * g + 1])[:, :cols].astype(BF16)
        qk_out[g] = qk
        v_out[g] = v
        mixed = [jnp.zeros((seq, cols), BF16)]
        for h in range(cols // HD):
            q = qk[:, h * HD : (h + 1) * HD]
            k = qk[:, cols + h * HD : cols + (h + 1) * HD]
            s = jnp.where(keys, nt(q, k) * (HD**-0.5), NEGATIVE)
            e = jnp.exp(s - jnp.max(s, axis=-1, keepdims=True))
            p = e * (1.0 / jnp.sum(e, axis=-1, keepdims=True))
            p = p.astype(BF16)
            soft_out[g * (cols // HD) + h] = p
            mixed.append(nn(p, v[:, h * HD : (h + 1) * HD]).astype(BF16))
        mixed = jnp.concatenate(mixed, axis=1)
        mixed_out[g] = mixed
        total = total + nt(mixed, weights[2 * g + 1])
    resid[...] = total
    xhat, _ = norm_parts(total)
    second[...] = (xhat * gain2[...]).astype(BF16)


def gate_softmax(second, router, experts):
    logits = nn(second, router)
    lane = lax.broadcasted_iota(jnp.int32, logits.shape, 1)
    logits = jnp.where(lane < experts, logits, NEGATIVE)
    e = jnp.exp(logits - jnp.max(logits, axis=-1, keepdims=True))
    return e / jnp.sum(e, axis=-1, keepdims=True)


def normal_cdf_pdf(x):
    return 0.5 + 0.5 * lax.erf(x * 0.5**0.5), jnp.exp(-0.5 * x * x) * 0.3989422804014327


def expert_kernel(layout, rows, count, experts, images, parts, seq_len, blocks, n_out, offs, router, *rest):
    sn = rest[:images]
    cot = rest[images : images + images * parts]
    at = images + images * parts
    live = rest[at]
    pieces = rest[at + 1 : at + 1 + count]
    at += 1 + count
    gs_out = rest[at : at + images]
    br_out = rest[at + images : at + 2 * images]
    outs = rest[at + 2 * images : at + 2 * images + n_out]
    weights, x_all, c_all, x_turned, c_turned, dpre_all, hw_all, stage, gs_acc, br_acc, w_acc, g_acc, stage_sems, sems = rest[
        at + 2 * images + n_out :
    ]
    seq = sn[0].shape[0]
    copies = {}
    number = 0
    for e in range(experts):
        for i in (e, experts + e):
            for array, src, lo, n, rel in layout:
                if lo <= i < lo + n:
                    spot = pl.multiple_of(offs[rel], 16)
                    copy = pltpu.make_async_copy(
                        pieces[array].at[src + i - lo], weights.at[i, pl.ds(spot, rows), :], sems.at[number]
                    )
                    number += 1
                    copy.start()
                    copies.setdefault(e, []).append(copy)
    for j in range(images):
        x_all[pl.ds(j * seq, seq), :] = sn[j][...]
        spot = j * seq
        for part in cot[j * parts : (j + 1) * parts]:
            c_all[pl.ds(spot, part.shape[0]), :] = part[...]
            spot += part.shape[0]
    x_turned[...] = x_all[...].T
    c_turned[...] = c_all[...].T
    going = []
    for e in range(experts):
        for copy in copies[e]:
            copy.wait()
        x = x_all[...]
        if e == 0:
            w = gate_softmax(x, router[...], experts) * live[...].astype(F32)
            w_acc[...] = w
            g_prev = jnp.zeros(w.shape, F32)
        else:
            w = w_acc[...]
            g_prev = g_acc[...]
        we = w[:, e : e + 1]
        lane = lax.broadcasted_iota(jnp.int32, w.shape, 1)
        pre = nn(x, weights[e])
        gh = nn(c_all[...], weights[experts + e])
        cdf, pdf = normal_cdf_pdf(pre)
        hidden = (pre * cdf).astype(BF16).astype(F32)
        g = jnp.sum(hidden * gh, axis=-1, keepdims=True)
        hw = (hidden * we).astype(BF16)
        dpre = (gh * we * (cdf + pre * pdf)).astype(BF16)
        hw_all[...] = hw
        dpre_all[...] = dpre
        g_acc[...] = jnp.where((lane == e) | (lane == e + 4), g, g_prev)
        branch = nt(hw, weights[experts + e])
        gs = nt(dpre, weights[e])
        if e == 0:
            br_acc[...] = branch
            gs_acc[...] = gs
        else:
            br_acc[...] += branch
            gs_acc[...] += gs
        for i, left, right in ((e, x_turned, dpre_all), (experts + e, c_turned, hw_all)):
            stage[i] = nn(left[...], right[...]).astype(BF16)
            for n, (which, j, rel) in enumerate(blocks):
                spot = pl.multiple_of(offs[rel], 16)
                going.append(
                    pltpu.make_async_copy(
                        stage.at[i, pl.ds(spot, rows), :], outs[which].at[j, i], stage_sems.at[i, n]
                    )
                )
                going[-1].start()
    for j in range(images):
        here = pl.ds(j * seq, seq)
        g = g_acc[here, :].T[:8, :]
        row = lax.broadcasted_iota(jnp.int32, g.shape, 0)
        coarse = g.astype(BF16).astype(F32)
        gs_acc[pl.ds(j * seq + seq_len, 8), 0:seq] = jnp.where(row < 4, coarse, g - coarse)
        gs_out[j][...] = gs_acc[here, :].astype(BF16)
        br_out[j][...] = br_acc[here, :].astype(BF16)
    for copy in going:
        copy.wait()


def attention_backward(
    layout, rows, count, blocks, n_out, images, experts, seq_len,
    offs, tokens, gain1, gain2, resid, second, first, qk_in, v_in, mixed_in, soft_in, live, router, cot, *rest,
):
    gs_in = rest[:images]
    pieces = rest[images : images + count]
    at = images + count
    grad_tokens, small = rest[at : at + 2]
    at += 2
    outs = rest[at : at + n_out]
    weights, stage, stage_sems, sems = rest[at + n_out :]
    copies = start_pieces(layout, pieces, weights, offs, rows, sems)
    width = second.shape[1]
    seq = second.shape[0]
    gs = gs_in[0][...].astype(F32)
    for j in range(1, images):
        gs = gs + gs_in[j][...].astype(F32)
    shares = gs[seq_len : seq_len + 8, 0:seq]
    shares = jnp.concatenate([shares, jnp.zeros((LANES - 8, seq), F32)], axis=0).T
    shares = shares + jnp.concatenate([shares[:, 4:8], jnp.zeros((seq, LANES - 4), F32)], axis=1)
    lane = lax.broadcasted_iota(jnp.int32, shares.shape, 1)
    shares = jnp.where(lane < experts, shares, 0.0) * live[...].astype(F32)
    gs = jnp.where(lax.broadcasted_iota(jnp.int32, gs.shape, 0) < seq_len, gs, 0.0)
    sn = second[...]
    probs = gate_softmax(sn, router[...], experts)
    inner = jnp.sum(probs * shares, axis=-1, keepdims=True)
    grad_logits = (probs * (shares - inner)).astype(BF16)
    grad_router = tn(grad_logits, sn)[:8, :]
    gs = gs + nt(grad_logits, router[...])
    xhat, inverse = norm_parts(resid[...])
    gain2_row = jnp.sum(gs * xhat, axis=0, keepdims=True)
    grad_resid = cot[...].astype(F32) + norm_backward(xhat, inverse, gs, gain2[...])
    ga = grad_resid.astype(BF16)
    first_turned = first[...].T
    ga_turned = ga.T
    going = []

    def send_blocks(going, i):
        for n, (which, j, rel) in enumerate(blocks):
            spot = pl.multiple_of(offs[rel], 16)
            going.append(
                pltpu.make_async_copy(stage.at[i, pl.ds(spot, rows), :], outs[which].at[j, i], stage_sems.at[i, n])
            )
            going[-1].start()

    scale = HD**-0.5
    groups = weights.shape[0] // 2
    cols = weights.shape[2] // 2
    for copy in copies:
        copy.wait()
    grad_first = None
    for g in range(groups):
        gm = nn(ga, weights[2 * g + 1])[:, cols:].astype(BF16)
        qk = qk_in[g]
        v = v_in[g]
        grads_q, grads_k, grads_v = [], [], []
        for h in range(cols // HD):
            q = qk[:, h * HD : (h + 1) * HD]
            k = qk[:, cols + h * HD : cols + (h + 1) * HD]
            gh = gm[:, h * HD : (h + 1) * HD]
            p = soft_in[g * (cols // HD) + h]
            grads_v.append(tn(p, gh).astype(BF16))
            p = p.astype(F32)
            gp = nt(gh, v[:, h * HD : (h + 1) * HD])
            ds = (p * (gp - jnp.sum(p * gp, axis=-1, keepdims=True))).astype(BF16)
            grads_q.append((nn(ds, k) * scale).astype(BF16))
            grads_k.append((tn(ds, q) * scale).astype(BF16))
        gqk = jnp.concatenate(grads_q + grads_k, axis=1)
        gv = jnp.concatenate(grads_v + [jnp.zeros((seq, cols), BF16)], axis=1)
        stage[2 * g] = nn(first_turned, gqk).astype(BF16)
        send_blocks(going, 2 * g)
        stage[2 * g + 1] = (nn(first_turned, gv) + nn(ga_turned, mixed_in[g])).astype(BF16)
        send_blocks(going, 2 * g + 1)
        part = nt(gqk, weights[2 * g]) + nt(gv, weights[2 * g + 1])
        grad_first = part if grad_first is None else grad_first + part
    xhat, inverse = norm_parts(tokens[...].astype(F32))
    gain1_row = jnp.sum(grad_first * xhat, axis=0, keepdims=True)
    result = grad_resid + norm_backward(xhat, inverse, grad_first, gain1[...])
    grad_tokens[...] = result[:seq_len]
    row = lax.broadcasted_iota(jnp.int32, (8, width), 0)
    found = jnp.where(row < experts, grad_router, jnp.where(row == 6, gain1_row, jnp.where(row == 7, gain2_row, 0.0)))
    small[...] = jnp.concatenate([found[:, i : i + small.shape[1]] for i in range(0, width, small.shape[1])], axis=0)
    for copy in going:
        copy.wait()


def call(kernel, out_shape, scratch, flops, n_bytes, name, operands, n_any, n_any_out=0):
    total = len(operands)
    in_specs = [pl.BlockSpec(memory_space=pltpu.SMEM)]
    in_specs += [pl.BlockSpec(memory_space=pltpu.VMEM)] * (total - 1 - n_any)
    in_specs += [pl.BlockSpec(memory_space=pl.ANY)] * n_any
    out_specs = [pl.BlockSpec(memory_space=pltpu.VMEM)] * (len(out_shape) - n_any_out)
    out_specs += [pl.BlockSpec(memory_space=pl.ANY)] * n_any_out
    return pl.pallas_call(
        kernel,
        out_shape=out_shape,
        in_specs=in_specs,
        out_specs=out_specs,
        scratch_shapes=scratch,
        compiler_params=pltpu.CompilerParams(vmem_limit_bytes=VMEM_LIMIT),
        cost_estimate=pl.CostEstimate(flops=flops, bytes_accessed=n_bytes, transcendentals=0),
        name=name,
    )(*operands)


def call_experts(
    operands, layout, rows, n_arrays, experts, count, parts, seq, seq_len, width, ff, blocks, n_out, out_lead
):
    here = count * seq
    grads = [jax.ShapeDtypeStruct((out_lead, 2 * experts, rows, ff), BF16)] * n_out
    return call(
        functools.partial(
            expert_kernel, layout, rows, n_arrays, experts, count, parts, seq_len, blocks, n_out
        ),
        [jax.ShapeDtypeStruct((seq, width), BF16)] * (2 * count) + grads,
        [
            pltpu.VMEM((2 * experts, width, ff), BF16),
            pltpu.VMEM((here, width), BF16),
            pltpu.VMEM((here, width), BF16),
            pltpu.VMEM((width, here), BF16),
            pltpu.VMEM((width, here), BF16),
            pltpu.VMEM((here, ff), BF16),
            pltpu.VMEM((here, ff), BF16),
            pltpu.VMEM((2 * experts, width, ff), BF16),
            pltpu.VMEM((here, width), F32),
            pltpu.VMEM((here, width), F32),
            pltpu.VMEM((here, LANES), F32),
            pltpu.VMEM((here, LANES), F32),
            pltpu.SemaphoreType.DMA((2 * experts, len(blocks))),
            pltpu.SemaphoreType.DMA((sum(piece[3] for piece in layout),)),
        ],
        15_000_000_000, 20_000_000, "experts", operands, n_arrays, n_any_out=n_out,
    )


def call_attention_forward(operands, layout, rows, n_arrays, seq, width, cols, groups):
    return call(
        functools.partial(attention_forward, layout, rows, n_arrays),
        [
            jax.ShapeDtypeStruct((seq, width), F32),
            jax.ShapeDtypeStruct((seq, width), BF16),
            jax.ShapeDtypeStruct((seq, width), BF16),
            jax.ShapeDtypeStruct((groups, seq, 2 * cols), BF16),
            jax.ShapeDtypeStruct((groups, seq, cols), BF16),
            jax.ShapeDtypeStruct((groups, seq, 2 * cols), BF16),
            jax.ShapeDtypeStruct((groups * cols // HD, seq, seq), BF16),
        ],
        [pltpu.VMEM((2 * groups, width, 2 * cols), BF16), pltpu.SemaphoreType.DMA((len(layout),))],
        8_000_000_000, 10_000_000, "attention_forward", operands, n_arrays,
    )


def call_attention_backward(
    operands, layout, rows, n_arrays, blocks, n_out, images, experts, seq_len, width, cols, groups, out_lead
):
    return call(
        functools.partial(
            attention_backward, layout, rows, n_arrays, blocks, n_out, images, experts, seq_len
        ),
        [jax.ShapeDtypeStruct((seq_len, width), F32), jax.ShapeDtypeStruct((8 * width // (2 * cols), 2 * cols), F32)]
        + [jax.ShapeDtypeStruct((out_lead, 2 * groups, rows, 2 * cols), BF16)] * n_out,
        [
            pltpu.VMEM((2 * groups, width, 2 * cols), BF16),
            pltpu.VMEM((2 * groups, width, 2 * cols), BF16),
            pltpu.SemaphoreType.DMA((2 * groups, len(blocks))),
            pltpu.SemaphoreType.DMA((len(layout),)),
        ],
        16_000_000_000, 16_000_000, "attention_backward", operands, n_arrays, n_any_out=n_out,
    )


def on_device(
    tokens, gain_first, qkv_weight, out_weight, gain_second, router_weight,
    expert_in, expert_out, routes, slot_index, cotangent, *, dp, tensor,
):
    me = lax.axis_index("dp")
    z = lax.axis_index("tensor")
    _, seq_len, width = tokens.shape
    experts, own_rows, ff = expert_in.shape
    cols = qkv_weight.shape[2]
    seq = (seq_len + 8 + 15) // 16 * 16
    images = tensor
    split = dp == 8
    rel_count = 8 if split else 1
    rows = width // rel_count
    offs = ((me ^ jnp.arange(8, dtype=jnp.int32)) * rows) if split else jnp.zeros((8,), jnp.int32)
    offs = offs.astype(jnp.int32)
    blocks = (
        [(0, j, r) for j, r in enumerate(KEEP)] + [(1, j, r) for j, r in enumerate(SEND)]
        if split
        else [(0, 0, 0)]
    )
    n_out = 2 if split else 1
    out_lead = 4 if split else 1

    def pad_rows(x):
        return jnp.pad(x, ((0, seq - seq_len), (0, 0)))

    tok = pad_rows(tokens[0])
    cot = pad_rows(cotangent[0])
    g1 = gain_first.reshape(1, width)
    g2 = gain_second.reshape(1, width)
    router = jnp.pad(router_weight, ((0, 0), (0, LANES - experts)))

    own = jnp.stack(
        [
            jnp.concatenate([qkv_weight[0], qkv_weight[1]], axis=1),
            jnp.concatenate([qkv_weight[2], out_weight.T], axis=1),
        ]
    )
    z_pieces = [own] + [shift(own, "tensor", tensor, j) for j in range(1, tensor)]
    z_buffer = jnp.concatenate(z_pieces, axis=0)
    expert_own = jnp.concatenate([expert_in, jnp.swapaxes(expert_out, 1, 2)], axis=0)
    expert_near = near_dp(expert_own, dp)
    z_buffer = after(z_buffer, *expert_near)

    near_images = images // 2
    cot_go = after(cot, z_buffer)
    straight = [shift(cot_go, "tensor", tensor, j) for j in range(1, near_images + 1)]
    attn_arrays, attn_layout, attn_second = gather_dp(z_buffer, near_dp(z_buffer, dp), dp, straight)
    relayed = [shift(straight[-1], "tensor", tensor, j) for j in range(1, images - near_images)]
    cots = [[cot] + straight[:-1], straight[-1:] + relayed]

    groups = tensor
    resid, second, first, qk, v, mixed, soft = call_attention_forward(
        [offs, tok, g1, g2] + attn_arrays, attn_layout, rows, len(attn_arrays), seq, width, cols, groups
    )

    seconds = [second] + [shift(second, "tensor", tensor, j) for j in range(1, tensor)]
    live = (slot_index < CAP) & (jnp.arange(seq_len) < VALID)[None, :, None]
    expert_lane = jnp.arange(LANES)
    live = jnp.any((routes[..., None] == expert_lane) & live[..., None], axis=2).astype(BF16)
    live = jnp.pad(live, ((0, 0), (0, seq - seq_len), (0, 0)))
    live = jnp.concatenate([lax.dynamic_slice_in_dim(live, z ^ j, 1, 0)[0] for j in range(images)], axis=0)

    expert_arrays, expert_layout, _ = gather_dp(expert_own, expert_near, dp, attn_second, (second, *relayed))
    gs_parts, branch_parts, made = [], [], []
    for (begin, count), cot_parts in zip(((0, near_images), (near_images, images - near_images)), cots):
        outs = call_experts(
            [offs, router]
            + seconds[begin : begin + count]
            + cot_parts
            + [after(live[begin * seq : (begin + count) * seq], *gs_parts)]
            + expert_arrays,
            expert_layout, rows, len(expert_arrays), experts, count, len(cot_parts) // count, seq, seq_len, width, ff, blocks, n_out, out_lead,
        )
        gs_parts += outs[:count]
        branch_parts += outs[count : 2 * count]
        made.append(outs[2 * count :])
    gs_all = [gs_parts[0]] + [shift(gs_parts[j], "tensor", tensor, j) for j in range(1, tensor)]

    summed, on_way, _, near_sums = reduce_dp([m[0] for m in made], [m[-1] for m in made], dp)
    grads_in = summed[:experts]
    grads_out = jnp.swapaxes(summed[experts:], 1, 2)
    if split:
        gs_all[0] = after(gs_all[0], *on_way)

    outs = call_attention_backward(
        [offs, tok, g1, g2, resid, second, first, qk, v, mixed, soft, live[:seq], router, cot] + gs_all + attn_arrays,
        attn_layout, rows, len(attn_arrays), blocks, n_out, images, experts, seq_len, width, cols, groups, out_lead,
    )
    grad_tokens, small = outs[:2]
    outs = outs[2:]

    tied = lax.optimization_barrier(tuple(branch_parts) + tuple(gs_all))[: len(branch_parts)]
    branches = [shift(tied[j], "tensor", tensor, j) for j in range(1, tensor)]
    branch = tied[0].astype(F32)
    for other in branches:
        branch = branch + other.astype(F32)
    output = (resid + branch)[:seq_len].astype(BF16)

    send = after(outs[n_out - 1], *branches[:-1], *near_sums)
    part, _, small, _ = reduce_dp([outs[0]], [send], dp, small, branches[-1:])
    part_low = part.astype(BF16)
    total = part[:2]
    smalls = []
    for j in range(1, tensor):
        block, mine, other = shift_with(part_low[2 * j : 2 * j + 2], small, "tensor", tensor, j)
        total = total + block.astype(F32)
        smalls = (smalls or [mine]) + [other]
    while len(smalls) > 1:
        smalls = [a + b for a, b in zip(smalls[::2], smalls[1::2])]
    small = jnp.concatenate([smalls[0][i : i + 8] for i in range(0, smalls[0].shape[0], 8)], axis=1)
    grad_qkv = jnp.stack([total[0, :, :cols], total[0, :, cols:], total[1, :, :cols]])
    grad_out_weight = total[1, :, cols:].T
    return (
        output[None],
        grad_tokens[None],
        small[6],
        grad_qkv,
        grad_out_weight,
        small[7],
        small[:experts].T,
        grads_in,
        grads_out,
    )


def solution(mesh):
    sizes = dict(mesh.shape)
    return jax.shard_map(
        functools.partial(on_device, dp=sizes["dp"], tensor=sizes["tensor"]),
        mesh=mesh,
        in_specs=(
            P(("dp", "tensor"), None, None),
            P(),
            P(None, "dp", "tensor"),
            P("tensor", "dp"),
            P(),
            P(),
            P(None, "dp", "tensor"),
            P(None, "tensor", "dp"),
            P("dp", None, None),
            P("dp", None, None),
            P(("dp", "tensor"), None, None),
        ),
        out_specs=(
            P(("dp", "tensor"), None, None),
            P(("dp", "tensor"), None, None),
            P(),
            P(None, "dp", "tensor"),
            P("tensor", "dp"),
            P(),
            P(),
            P(None, "dp", "tensor"),
            P(None, "tensor", "dp"),
        ),
        check_vma=False,
    )
```
